256 devices in a mesh: phase: 16 (over x_hi, z), dp: 16 (over x_lo, y, core).
Axes of the slice: x: 4 (x_hi: 2, x_lo: 2; x = x_hi * 2 + x_lo), y: 4, z: 8, core: 2. Of those that a mesh axis runs over, the one named last changes fastest.
Arguments:
- hidden_flight: bfloat16 [16, 16, 48, 1536], P('phase', 'dp'), may hold values from -6 to 6
- latent_flight: bfloat16 [16, 16, 48, 64], P('phase', 'dp'), may hold values from -6 to 6
- key_cache: bfloat16 [16, 32, 256, 1536], P('phase', 'dp'), may hold values from -97 to 97
- value_cache: bfloat16 [16, 32, 256, 1536], P('phase', 'dp'), may hold values from -6 to 6
- text_keys: bfloat16 [16, 32, 256, 1536], P('phase', 'dp'), may hold values from -9 to 9
- text_values: bfloat16 [16, 32, 256, 1536], P('phase', 'dp'), may hold values from -6 to 6
- norm_gain: float32 [16, 1536], P('phase'), may hold values from 0.1 to 1.9
- w_qkv: bfloat16 [16, 1536, 4608], P('phase', 'dp'), may hold values from -0.15625 to 0.15625
- w_out: bfloat16 [16, 1536, 1536], P('phase', 'dp'), may hold values from -0.15625 to 0.15625
- embed_weight: bfloat16 [64, 1536], replicated, may hold values from -0.75 to 0.75
- embed_bias: float32 [1536], replicated, may hold values from -6 to 6
- head_weight: bfloat16 [1536, 64], replicated, may hold values from -0.21875 to 0.21875
- head_bias: float32 [64], replicated, may hold values from -6 to 6
- sigma_table: float32 [5], replicated, may hold values from 0 to 1, as said below
- step_index: int32 [32], P('dp'), may hold values from 0 to 3
- patch_lengths: int32 [32, 8], P('dp'), may hold values from 1 to 48, 256 in all within a row
Outputs:
- hidden_out: bfloat16 [16, 16, 48, 1536], P('phase', 'dp')
- latent_out: bfloat16 [16, 16, 48, 64], P('phase', 'dp')
- key_out: bfloat16 [16, 32, 256, 1536], P('phase', 'dp')
- value_out: bfloat16 [16, 32, 256, 1536], P('phase', 'dp')
The draws below stay inside these ranges and needn't reach their ends.
Inputs may be any that keep to these rules, and one draw needn't show every extreme that they name: `patch_lengths`: the 8 lengths of one image sum to 256, and the longest of each image is exactly 48. `sigma_table`: entry 0 is 1, entry 4 is 0, and the entries fall from one to the next.
All inputs are finite; a program needn't handle non-finite values.
Results may differ from the reference program's by a relative error of at most 0.039.
Values may be sent and summed in bfloat16 or wider, within the bound.
No kernel may reach another device: no remote copies, remote signals or barrier semaphores. Data moves between devices by JAX's collectives and lax.ppermute only.
A program may use at most 128 MiB of HBM per device.

```python
import math
import jax
import jax.numpy as jnp
import numpy as np
from jax import lax

D = 1536
HEAD_DIM = 128
CL = 64
PATCHES = 8
TICKS = 3
STEPS = 4
IMG_TOK = 256
TXT = 256
INNER = 1536
CAP = 48
IMAGES = 32
N_PHASE = 16
N_DP = 16


def draw_key_cache(key, part):
    key = jax.random.fold_in(key, 11)
    shape = (N_PHASE, IMAGES, IMG_TOK, INNER)
    drawn = 1.5 * jax.random.normal(key, shape, jnp.float32)
    return drawn.astype(jnp.bfloat16)


def draw_sigma_table(key, part):
    key = jax.random.fold_in(key, 7)
    increments = jnp.exp(jax.random.uniform(key, (STEPS,), jnp.float32, -1.2, 1.2))
    covered = jnp.concatenate([jnp.zeros((1,), jnp.float32), jnp.cumsum(increments)])
    return 1.0 - covered / covered[-1]


def plant(values, key, least, high):
    longest = values.shape.index(max(values.shape))
    spots = []
    for shift in (0, 1):
        where = [jax.random.randint(jax.random.fold_in(key, axis), (), 0, length) for axis, length in enumerate(values.shape)]
        where[longest] = (where[longest] + shift) % values.shape[longest]
        spots.append(tuple(where))
    return values.at[spots[0]].set(least).at[spots[1]].set(high)


def steps_of(key, extent, cuts, low, top_value):
    factor_of, own = 1.0, jax.random.fold_in(key, 6)
    for axis_at, parts in cuts:
        steps = jnp.exp(jax.random.uniform(jax.random.fold_in(own, axis_at), (parts,), jnp.float32, low / len(cuts), top_value / len(cuts)))
        factor_of = factor_of * jnp.repeat(steps, extent[axis_at] // parts).reshape([-1 if axis == axis_at else 1 for axis in range(len(extent))])
    return factor_of


def split_up(number_of, total, bound, slope):
    loads = [(1 << 20) // math.isqrt(standing ** slope) + 1 for standing in range(2, number_of + 1)]
    rest, holding = total - bound - (number_of - 1), [1] * (number_of - 1)
    while rest > 0:
        movable = [i for i in range(number_of - 1) if holding[i] < bound]
        pool, budget = sum([loads[i] for i in movable]), rest
        for i in movable:
            more = min(bound - holding[i], max(1, budget * loads[i] // pool), rest)
            holding[i] = holding[i] + more
            rest = rest - more
    return np.array([bound] + holding)


def uneven(own_key, count, total, most, lean):
    if count == 2:
        one = jax.random.randint(own_key, (), max(1, total - most), min(most, total - 1) + 1)
        return jnp.stack([one, total - one])
    sizes = jnp.asarray(split_up(count, total, most, lean), jnp.int32)
    pairs = (count - 1) // 2
    giver, sink = sizes[1:1 + 2 * pairs:2], sizes[2:2 + 2 * pairs:2]
    room = jnp.minimum(giver - 1, most - sink)
    passed = jax.random.randint(jax.random.fold_in(own_key, 1), (pairs,), 0, 1 << 20) % (room + 1)
    sizes = sizes.at[1:1 + 2 * pairs:2].set(giver - passed).at[2:2 + 2 * pairs:2].set(sink + passed)
    return sizes[jax.random.permutation(jax.random.fold_in(own_key, 2), count)]


def noise(key, dims, width, most, cuts=(), kind=jnp.bfloat16):
    values = width * jax.random.normal(key, dims, jnp.float32)
    if cuts:
        values = values * steps_of(key, dims, cuts, -0.22, 0.18)
    return jnp.clip(values, -most, most).astype(kind)


def setup_inputs(seed: int = 0) -> dict:
    splits = jax.random.split(jax.random.key(seed), 17)
    hidden_flight = noise(splits[0], (N_PHASE, N_DP, CAP, D), 1.0, 6.0, ((0, 16), (1, 16)))
    latent_flight = noise(splits[1], (N_PHASE, N_DP, CAP, CL), 1.0, 6.0, ((0, 16), (1, 16)))
    key_cache = draw_key_cache(jax.random.fold_in(splits[16], 71), 0)
    value_cache = noise(splits[3], (N_PHASE, IMAGES, IMG_TOK, INNER), 1.0, 6.0, ((0, 16), (1, 16)))
    text_keys = noise(splits[4], (N_PHASE, IMAGES, TXT, INNER), 1.5, 9.0, ((0, 16), (1, 16)))
    text_values = noise(splits[5], (N_PHASE, IMAGES, TXT, INNER), 1.0, 6.0, ((0, 16), (1, 16)))
    norm_gain = jnp.clip(1.0 + 0.18 * jax.random.normal(splits[6], (N_PHASE, D), jnp.float32), 0.1, 1.9)
    w_qkv = noise(splits[7], (N_PHASE, D, 3 * INNER), D ** -0.5, 0.15625, ((0, 16), (1, 16)))
    w_out = noise(splits[8], (N_PHASE, INNER, D), INNER ** -0.5, 0.15625, ((0, 16), (1, 16)))
    embed_weight = noise(splits[9], (CL, D), CL ** -0.5, 0.75)
    embed_bias = noise(splits[10], (D,), 1.0, 6.0, (), jnp.float32)
    head_weight = noise(splits[11], (D, CL), (D // 2) ** -0.5, 0.21875)
    head_bias = noise(splits[12], (CL,), 1.0, 6.0, (), jnp.float32)
    sigma_table = draw_sigma_table(jax.random.fold_in(splits[16], 71), 0)
    step_index = plant(jax.random.randint(splits[14], (IMAGES,), 0, STEPS), jax.random.fold_in(splits[14], 1), 0, STEPS - 1).astype(jnp.int32)
    patch_lengths = jax.vmap(lambda own: uneven(own, PATCHES, IMG_TOK, CAP, 1))(jax.random.split(splits[15], IMAGES)).reshape((IMAGES, PATCHES)).astype(jnp.int32)
    return dict(hidden_flight=hidden_flight, latent_flight=latent_flight, key_cache=key_cache, value_cache=value_cache, text_keys=text_keys, text_values=text_values, norm_gain=norm_gain, w_qkv=w_qkv, w_out=w_out, embed_weight=embed_weight, embed_bias=embed_bias, head_weight=head_weight, head_bias=head_bias, sigma_table=sigma_table, step_index=step_index, patch_lengths=patch_lengths)


epsilon = 1e-06

def normalize(row_block):
    widened = row_block.astype(jnp.float32)
    return widened * lax.rsqrt(lax.optimization_barrier(jnp.mean(widened * widened, axis=-1, keepdims=True)) + epsilon)

def place_rows(cached, fresh_rows, offset, inside):
    token_count = cached.shape[0]
    canvas = jnp.zeros((token_count + fresh_rows.shape[0], fresh_rows.shape[1]), fresh_rows.dtype)
    canvas = lax.dynamic_update_slice_in_dim(canvas, fresh_rows, offset.astype(jnp.int32), 0)
    return jnp.where(inside[:, None], canvas[:token_count], cached)

def attend(queries, key_rows, value_rows, allowed):
    row_count = queries.shape[0]
    inner_width = queries.shape[1]
    head_count = inner_width // HEAD_DIM
    query_heads = queries.astype(jnp.float32).reshape(row_count, head_count, HEAD_DIM)
    key_heads = key_rows.astype(jnp.float32).reshape(key_rows.shape[0], head_count, HEAD_DIM)
    value_heads = value_rows.astype(jnp.float32).reshape(value_rows.shape[0], head_count, HEAD_DIM)
    scores = jnp.einsum('qhd,khd->hqk', query_heads, key_heads) * (1.0 / math.sqrt(HEAD_DIM))
    scores = jnp.where(allowed[None, None, :], scores, -jnp.inf)
    highest = lax.optimization_barrier(jnp.max(scores, axis=-1, keepdims=True))
    raised = jnp.exp(scores - highest)
    attn_weights = (raised / lax.optimization_barrier(jnp.sum(raised, axis=-1, keepdims=True))).astype(jnp.bfloat16)
    attended = jnp.einsum('hqk,khd->qhd', attn_weights.astype(jnp.float32), value_heads)
    return attended.reshape(row_count, inner_width).astype(jnp.bfloat16)

def reference(hidden_flight, latent_flight, key_cache, value_cache, text_keys, text_values, norm_gain, w_qkv, w_out, embed_weight, embed_bias, head_weight, head_bias, sigma_table, step_index, patch_lengths):
    sections = N_PHASE
    columns = N_DP
    per_column = sections // PATCHES
    capacity = hidden_flight.shape[2]
    inner_width = w_out.shape[1]
    offsets = (jnp.cumsum(patch_lengths, axis=1) - patch_lengths).astype(jnp.int32)
    lengths = patch_lengths.reshape(columns, per_column, PATCHES)
    offsets = offsets.reshape(columns, per_column, PATCHES)
    sigma_jumps = (sigma_table[step_index + 1] - sigma_table[step_index]).reshape(columns, per_column)

    def by_column(cache):
        return cache.reshape(sections, columns, per_column, cache.shape[2], cache.shape[3])
    keys_img = by_column(key_cache)
    values_img = by_column(value_cache)
    keys_txt = by_column(text_keys)
    values_txt = by_column(text_values)
    row_ids = jnp.arange(capacity)
    token_ids = jnp.arange(key_cache.shape[2])
    text_ok = jnp.ones((text_keys.shape[2],), bool)
    hidden = hidden_flight
    latents = latent_flight
    for instant in range(TICKS):

        def one_section(packed):
            section, sec_hidden, sec_latents, sec_keys, sec_values, sec_text_k, sec_text_v, sec_gain, sec_qkv, sec_out = packed
            flight_slot = jnp.mod(instant - section, sections)
            picture = flight_slot // PATCHES
            segment = flight_slot % PATCHES

            def one_column(col_hidden, col_latents, col_keys, col_values, col_text_k, col_text_v, col_lengths, col_offsets, col_jumps):
                length = col_lengths[picture, segment]
                offset = col_offsets[picture, segment]
                live_rows = row_ids < length
                inside = (token_ids >= offset) & (token_ids < offset + length)
                normed = (normalize(col_hidden) * sec_gain).astype(jnp.bfloat16)
                projected = jnp.dot(normed, sec_qkv, preferred_element_type=jnp.float32).astype(jnp.bfloat16)
                queries = projected[:, :inner_width]
                fresh_k = projected[:, inner_width:2 * inner_width]
                fresh_v = projected[:, 2 * inner_width:]
                cached_k = col_keys[picture]
                cached_v = col_values[picture]
                allowed = jnp.concatenate([text_ok, jnp.logical_not(inside), live_rows])
                attended = attend(queries, jnp.concatenate([col_text_k[picture], cached_k, fresh_k], 0), jnp.concatenate([col_text_v[picture], cached_v, fresh_v], 0), allowed)
                summed = col_hidden.astype(jnp.float32) + jnp.dot(attended, sec_out, preferred_element_type=jnp.float32)
                hidden_new = jnp.where(live_rows[:, None], summed, 0.0).astype(jnp.bfloat16)
                keys_new = col_keys.at[picture].set(place_rows(cached_k, fresh_k, offset, inside))
                values_new = col_values.at[picture].set(place_rows(cached_v, fresh_v, offset, inside))
                velocity = jnp.dot(normalize(hidden_new).astype(jnp.bfloat16), head_weight, preferred_element_type=jnp.float32) + head_bias
                stepped = jnp.where(live_rows[:, None], col_latents.astype(jnp.float32) + col_jumps[picture] * velocity, 0.0).astype(jnp.bfloat16)
                latents_new = jnp.where(section == sections - 1, stepped, col_latents)
                return (hidden_new, latents_new, keys_new, values_new)
            return jax.vmap(one_column)(sec_hidden, sec_latents, sec_keys, sec_values, sec_text_k, sec_text_v, lengths, offsets, sigma_jumps)
        hidden_done, latents_done, keys_img, values_img = lax.map(one_section, (jnp.arange(sections), hidden, latents, keys_img, values_img, keys_txt, values_txt, norm_gain, w_qkv, w_out))
        hidden = jnp.roll(hidden_done, 1, axis=0)
        latents = jnp.roll(latents_done, 1, axis=0)
        arrival = (instant + 1) % sections
        arrival_len = lengths[:, arrival // PATCHES, arrival % PATCHES]
        embedded = jnp.dot(latents[0].reshape(columns * capacity, latents.shape[3]), embed_weight, preferred_element_type=jnp.float32)
        embedded = embedded.reshape(columns, capacity, embed_weight.shape[1]) + embed_bias
        keep_rows = row_ids[None, :] < arrival_len[:, None]
        embedded = jnp.where(keep_rows[:, :, None], embedded, 0.0).astype(jnp.bfloat16)
        hidden = hidden.at[0].set(embedded)
    return (hidden, latents, keys_img.reshape(key_cache.shape), values_img.reshape(value_cache.shape))
```

```python
import functools
import math

import jax
import jax.numpy as jnp
from jax import lax
from jax.experimental import pallas as pl
from jax.experimental.pallas import tpu as pltpu
from jax.sharding import PartitionSpec as P

HEAD_DIM = 128
TICKS = 3
WINDOW = 64
TILE = 16
GRANT = 12 * 1024 * 1024

epsilon = 1e-06

X, Y, C = 2, 4, 2


def spot(x, y, core):
    return ((x % X) * Y + (y % Y)) * C + core


def moved(value, dx, dy, dc):
    pairs = [
        (spot(x, y, c), spot(x + dx, y + dy, (c + dc) % C))
        for x in range(X)
        for y in range(Y)
        for c in range(C)
    ]
    return lax.ppermute(value, "dp", pairs)


def shifted(value):
    count = lax.axis_size("phase")
    pairs = [(source, (source + 1) % count) for source in range(count)]
    return lax.ppermute(value, "phase", pairs)


def joined(*values):
    return lax.optimization_barrier(values)


NEAR = [
    (0, 0, 0, 16),
    (0, -1, 0, 8),
    (0, -1, 8, 8),
    (0, 1, 0, 8),
    (0, 1, 8, 8),
    (1, 0, 0, 8),
    (1, 0, 8, 8),
]
MIDDLE = [(0, 2, 0, 8), (0, 2, 8, 8), (1, -1, 0, 8), (1, 1, 0, 8), (1, 2, 0, 8)]
LAST = [(1, -1, 8, 8), (1, 1, 8, 8), (1, 2, 8, 8)]


def in_hbm(array):
    return pltpu.with_memory_space_constraint(array, pltpu.HBM)


def pair(piece):
    return moved(piece, 0, 0, 1)


def places(rows, group):
    device = lax.axis_index("dp")
    core = lax.rem(device, C)
    y = lax.rem(device // C, Y)
    x = device // (C * Y)
    found = []
    for dx, dy, dc, part, count in group:
        source = (lax.rem(x + dx, X) * Y + lax.rem(y + dy + Y, Y)) * C + lax.rem(core + dc, C)
        found.append((pl.multiple_of(source * rows + part * rows // 16, TILE), count * rows // 16))
    return found


def both(group):
    return [(dx, dy, dc, part, count) for dc in range(C) for dx, dy, part, count in group]


def normalize(widened):
    return widened * lax.rsqrt(jnp.mean(widened * widened, axis=-1, keepdims=True) + epsilon)


def batch_of(tick, section, sections, lengths_ref):
    patches = lengths_ref.shape[1]
    slot = lax.rem(tick - section + sections, sections)
    picture = slot // patches
    segment = lax.rem(slot, patches)
    length = lengths_ref[picture, segment]
    offset = jnp.int32(0)
    for m in range(patches - 1):
        offset = offset + jnp.where(m < segment, lengths_ref[picture, m], 0)
    return picture, length, offset


def embedded_rows(latents, embed_w_ref, embed_b_ref, live):
    rows = jnp.dot(latents, embed_w_ref[...], preferred_element_type=jnp.float32) + embed_b_ref[...][None]
    row_ids = lax.broadcasted_iota(jnp.int32, rows.shape, 0)
    return jnp.where(row_ids < live, rows, 0.0).astype(jnp.bfloat16)


def attend(proj, image_k, image_v, text_k, text_v, attended):
    width = attended.shape[1]
    scale = 1.0 / math.sqrt(HEAD_DIM)
    across = (((1,), (1,)), ((), ()))
    for head in range(width // HEAD_DIM):
        cols = slice(head * HEAD_DIM, (head + 1) * HEAD_DIM)
        queries = proj[:, cols]
        on_text = lax.dot_general(queries, text_k[:, cols], across, preferred_element_type=jnp.float32)
        on_image = lax.dot_general(queries, image_k[:, cols], across, preferred_element_type=jnp.float32)
        highest = jnp.maximum(
            jnp.max(on_text, axis=-1, keepdims=True), jnp.max(on_image, axis=-1, keepdims=True)
        )
        on_text = jnp.exp((on_text - highest) * scale)
        on_image = jnp.exp((on_image - highest) * scale)
        total = jnp.sum(on_text, axis=-1, keepdims=True) + jnp.sum(on_image, axis=-1, keepdims=True)
        mixed = jnp.dot(
            on_text.astype(jnp.bfloat16), text_v[:, cols], preferred_element_type=jnp.float32
        ) + jnp.dot(on_image.astype(jnp.bfloat16), image_v[:, cols], preferred_element_type=jnp.float32)
        attended[:, cols] = (mixed / total).astype(jnp.bfloat16)


def weight_copies(pieces, weights, rows, group, sems):
    return [
        pltpu.make_async_copy(piece, weights.at[pl.ds(start, count), :], sems.at[at])
        for at, (piece, (start, count)) in enumerate(zip(pieces, places(rows, group)))
    ]


def run_copies(copies):
    for copy in copies:
        copy.start()
    for copy in copies:
        copy.wait()


def own_kernel(qkv, out, low, high, whole, sems):
    half, width = low.shape[0], qkv.shape[1]
    copies = []
    for at, (target, start) in enumerate(((low, 0), (high, half), (whole, 0))):
        rows = pl.ds(start, target.shape[0])
        copies += [
            pltpu.make_async_copy(qkv.at[rows, :], target.at[:, pl.ds(0, width)], sems.at[2 * at]),
            pltpu.make_async_copy(
                out.at[rows, :], target.at[:, pl.ds(width, out.shape[1])], sems.at[2 * at + 1]
            ),
        ]
    run_copies(copies)


def load_kernel(rows, group, copied, first, *refs):
    if not first:
        refs = refs[1:]
    count = len(group)
    pieces, sources, refs = refs[:count], refs[count : count + copied], refs[count + copied :]
    weights, targets, (sems, copy_sems) = refs[0], refs[1 : 1 + copied], refs[1 + copied :]
    run_copies(
        weight_copies(pieces, weights, rows, group, sems)
        + [
            pltpu.make_async_copy(source, target, copy_sems.at[at])
            for at, (source, target) in enumerate(zip(sources, targets))
        ]
    )


def tick_kernel(tick, sections, first, rows, *refs):
    lengths, steps, sigmas = refs[:3]
    gain, embed_w, embed_b, head_w, head_b = refs[3:8]
    text_k, text_v, keys_in, values_in = refs[8:12]
    rest = refs[12:]
    if first:
        hidden_in, latents_in, _ = rest[:3]
        pieces = rest[3 : 3 + C * len(LAST)]
        keys, values, weights, sent, *scratch = rest[3 + C * len(LAST) :]
    else:
        received, weights = rest[:2]
        keys, values, sent, *scratch = rest[2:]
    hidden, image_k, image_v, txt_k, txt_v, proj, attended, cache_sem, back_sem, *weight_sem = scratch
    width = hidden.shape[1]
    section = lax.axis_index("phase")
    picture, length, offset = batch_of(tick, section, sections, lengths)
    base = pl.multiple_of(jnp.minimum((offset // TILE) * TILE, image_k.shape[0] - WINDOW), TILE)

    loads = [
        pltpu.make_async_copy(source.at[picture], target, cache_sem.at[at])
        for at, (source, target) in enumerate(
            [(keys_in, image_k), (values_in, image_v), (text_k, txt_k), (text_v, txt_v)]
        )
    ]
    weight_loads = []
    if first:
        weight_loads = weight_copies(pieces, weights, rows, both(LAST), weight_sem[0])
    for load in weight_loads + loads:
        load.start()

    if first:
        hidden[...] = hidden_in[...]
    else:
        hidden[...] = received[:, :width]

        @pl.when(section == 0)
        def _():
            hidden[...] = embedded_rows(
                received[:, width : width + embed_w.shape[0]], embed_w, embed_b, lengths[0, tick]
            )

    normed = (normalize(hidden[...].astype(jnp.float32)) * gain[...]).astype(jnp.bfloat16)
    for load in weight_loads:
        load.wait()
    for block in range(3):
        cols = slice(block * width, (block + 1) * width)
        proj[:, cols] = jnp.dot(normed, weights[:, cols], preferred_element_type=jnp.float32).astype(
            jnp.bfloat16
        )
    for load in loads:
        load.wait()

    token = lax.broadcasted_iota(jnp.int32, (WINDOW, proj.shape[0]), 0) + base - offset
    place = (token == lax.broadcasted_iota(jnp.int32, token.shape, 1)) & (token < length)
    place = place.astype(jnp.bfloat16)
    token = lax.broadcasted_iota(jnp.int32, (WINDOW, width), 0) + base - offset
    inside = (token >= 0) & (token < length)
    for block, cache in ((1, image_k), (2, image_v)):
        fresh = jnp.dot(
            place, proj[:, block * width : (block + 1) * width], preferred_element_type=jnp.float32
        )
        old = cache[pl.ds(base, WINDOW), :].astype(jnp.float32)
        cache[pl.ds(base, WINDOW), :] = jnp.where(inside, fresh, old).astype(jnp.bfloat16)
    backs = [
        pltpu.make_async_copy(
            source.at[pl.ds(base, WINDOW), :],
            target.at[picture, pl.ds(base, WINDOW), :],
            back_sem.at[at],
        )
        for at, (source, target) in enumerate([(image_k, keys), (image_v, values)])
    ]
    for back in backs:
        back.start()

    attend(proj, image_k, image_v, txt_k, txt_v, attended)

    summed = hidden[...].astype(jnp.float32) + jnp.dot(
        attended[...], weights[:, 3 * width :], preferred_element_type=jnp.float32
    )
    row_ids = lax.broadcasted_iota(jnp.int32, summed.shape, 0)
    hidden_new = jnp.where(row_ids < length, summed, 0.0).astype(jnp.bfloat16)
    sent[:, :width] = hidden_new
    channels = embed_w.shape[0]
    latents = latents_in[...] if first else received[:, width : width + channels]
    sent[:, width:] = jnp.concatenate(
        [latents, jnp.zeros((latents.shape[0], sent.shape[1] - width - channels), latents.dtype)], axis=1
    )

    @pl.when(section == sections - 1)
    def _():
        velocity = (
            lax.dot_general(
                normalize(hidden_new.astype(jnp.float32)).astype(jnp.bfloat16),
                head_w[...],
                (((1,), (1,)), ((), ())),
                preferred_element_type=jnp.float32,
            )
            + head_b[...][None]
        )
        step = steps[picture]
        jump = sigmas[step + 1] - sigmas[step]
        stepped = latents.astype(jnp.float32) + jump * velocity
        row_ids = lax.broadcasted_iota(jnp.int32, stepped.shape, 0)
        stepped = jnp.where(row_ids < length, stepped, 0.0).astype(jnp.bfloat16)
        sent[:, width:] = jnp.concatenate(
            [stepped, jnp.zeros((latents.shape[0], sent.shape[1] - width - channels), latents.dtype)],
            axis=1,
        )

    for back in backs:
        back.wait()


def final_kernel(tick, lengths, embed_w, embed_b, received, hidden, latents):
    width = hidden.shape[1]
    arrived = received[:, width : width + latents.shape[1]]
    hidden[...] = received[:, :width]
    latents[...] = arrived

    @pl.when(lax.axis_index("phase") == 0)
    def _():
        hidden[...] = embedded_rows(arrived, embed_w, embed_b, lengths[0, tick])


def shards(
    hidden_flight,
    latent_flight,
    key_cache,
    value_cache,
    text_keys,
    text_values,
    norm_gain,
    w_qkv,
    w_out,
    embed_weight,
    embed_bias,
    head_weight,
    head_bias,
    sigma_table,
    step_index,
    patch_lengths,
):
    sections = lax.axis_size("phase")
    hidden = hidden_flight[0, 0]
    latents = latent_flight[0, 0]
    keys, values = key_cache[0], value_cache[0]
    rows, width = hidden.shape
    wide = width + HEAD_DIM
    tokens = keys.shape[1]
    part = w_qkv.shape[1]
    full = part * lax.axis_size("dp")
    smem = pl.BlockSpec(memory_space=pltpu.SMEM)
    vmem = pl.BlockSpec(memory_space=pltpu.VMEM)
    hbm = pl.BlockSpec(memory_space=pl.ANY)
    scalars = [patch_lengths, step_index, sigma_table]
    small = [norm_gain, embed_weight, embed_bias, head_weight.T, head_bias]
    texts = [text_keys[0], text_values[0]]
    params = pltpu.CompilerParams(vmem_limit_bytes=GRANT)
    small_params = pltpu.CompilerParams(vmem_limit_bytes=GRANT // 8)

    full = part * lax.axis_size("dp")
    total = w_qkv.shape[2] + w_out.shape[2]
    halves = [jax.ShapeDtypeStruct((part // 2, total), jnp.bfloat16)] * 2
    low, high, whole = pl.pallas_call(
        own_kernel,
        out_shape=halves + [jax.ShapeDtypeStruct((part, total), jnp.bfloat16)],
        in_specs=[hbm] * 2,
        out_specs=[hbm] * 3,
        scratch_shapes=[pltpu.SemaphoreType.DMA((6,))],
        compiler_params=small_params,
        name="own",
    )(in_hbm(w_qkv[0]), in_hbm(w_out[0]))

    def loaded(weights, pieces, group, copied, name):
        first = weights is None
        if not first:
            weights = pltpu.with_memory_space_constraint(weights, pltpu.VMEM)
        return pl.pallas_call(
            functools.partial(load_kernel, part, group, len(copied), first),
            out_shape=[pltpu.VMEM((full, total), jnp.bfloat16)]
            + [jax.ShapeDtypeStruct(array.shape, array.dtype) for array in copied],
            in_specs=[vmem] * (not first) + [hbm] * (len(pieces) + len(copied)),
            out_specs=[vmem] + [hbm] * len(copied),
            scratch_shapes=[
                pltpu.SemaphoreType.DMA((len(pieces),)),
                pltpu.SemaphoreType.DMA((max(len(copied), 1),)),
            ],
            input_output_aliases={} if first else {0: 0},
            compiler_params=small_params,
            name=name,
        )(*([] if first else [weights]), *pieces, *[in_hbm(array) for array in copied])

    below_low, above_high, across_low = moved(low, 0, 1, 0), moved(high, 0, -1, 0), moved(low, 1, 0, 0)
    below_high, above_low = moved(high, 0, 1, 0), moved(low, 0, -1, 0)
    far_low, far_high = moved(below_low, 0, 1, 0), moved(above_high, 0, -1, 0)
    across_high = moved(joined(high, across_low)[0], 1, 0, 0)
    ready = joined(whole, below_low, above_high, across_low, below_high, below_high, above_low, across_high)
    whole_pair, below_low_pair, above_high_pair, across_low_pair, below_high_pair = [pair(piece) for piece in ready[:5]]
    far_low, far_high, onward_low, onward_high, *ready = joined(
        far_low, far_high, across_low, across_high, above_low, across_high, whole_pair, below_low_pair, above_high_pair, across_low_pair, below_high_pair
    )
    above_low_pair, across_high_pair = [pair(piece) for piece in ready[:2]]
    xu_low, xd_low, xf_low = moved(onward_low, 0, 1, 0), moved(onward_low, 0, -1, 0), moved(far_low, 1, 0, 0)
    xu_high, xd_high, xf_high = moved(onward_high, 0, 1, 0), moved(onward_high, 0, -1, 0), moved(far_high, 1, 0, 0)
    near = [whole, below_low, below_high, above_low, above_high, across_low, across_high]
    near += [whole_pair, below_low_pair, below_high_pair, above_low_pair, above_high_pair, across_low_pair, across_high_pair]
    weights, keys, values = loaded(None, near, both(NEAR), [keys, values], "near")
    low_set = [far_low, far_high, xu_low, xd_low, xf_low]
    keys, *low_set = joined(keys, *low_set)
    middle = low_set + [pair(piece) for piece in low_set]
    weights, latents = loaded(weights, middle, both(MIDDLE), [latents], "middle")
    latents, *last = joined(latents, xu_high, xd_high, xf_high)
    last += [pair(piece) for piece in last]

    for tick in range(TICKS):
        first = tick == 0
        weights = pltpu.with_memory_space_constraint(weights, pltpu.VMEM)
        if first:
            own = [hidden, latents, weights] + last
            own_specs = [vmem] * 3 + [hbm] * len(last)
        else:
            own = [received, weights]
            own_specs = [vmem] * 2
        shapes = [
            jax.ShapeDtypeStruct(keys.shape, keys.dtype),
            jax.ShapeDtypeStruct(values.shape, values.dtype),
        ]
        out_specs = [hbm, hbm]
        aliases = {10: 0, 11: 1}
        if first:
            shapes.append(pltpu.VMEM(weights.shape, weights.dtype))
            out_specs.append(vmem)
            aliases[14] = 2
        shapes.append(jax.ShapeDtypeStruct((rows, wide), jnp.bfloat16))
        out_specs.append(vmem)
        scratch = [
            pltpu.VMEM((rows, width), jnp.bfloat16),
            *[pltpu.VMEM((tokens, width), jnp.bfloat16)] * 4,
            pltpu.VMEM((rows, 3 * width), jnp.bfloat16),
            pltpu.VMEM((rows, width), jnp.bfloat16),
            pltpu.SemaphoreType.DMA((4,)),
            pltpu.SemaphoreType.DMA((2,)),
        ]
        if first:
            scratch.append(pltpu.SemaphoreType.DMA((len(last),)))
        results = pl.pallas_call(
            functools.partial(tick_kernel, tick, sections, first, part),
            out_shape=shapes,
            in_specs=[smem] * 3 + [vmem] * 5 + [hbm] * 4 + own_specs,
            out_specs=out_specs,
            scratch_shapes=scratch,
            input_output_aliases=aliases,
            compiler_params=params,
            name=f"tick{tick}",
        )(*scalars, *small, *texts, keys, values, *own)
        if first:
            keys, values, weights, sent = results
        else:
            keys, values, sent = results
        received = shifted(sent)

    hidden, latents = pl.pallas_call(
        functools.partial(final_kernel, TICKS),
        out_shape=[
            jax.ShapeDtypeStruct(hidden.shape, hidden.dtype),
            jax.ShapeDtypeStruct(latents.shape, latents.dtype),
        ],
        in_specs=[smem, vmem, vmem, vmem],
        out_specs=[vmem, vmem],
        compiler_params=params,
        name="final",
    )(patch_lengths, embed_weight, embed_bias, received)
    return (hidden[None, None], latents[None, None], keys[None], values[None])


def solution(mesh):
    placed = (
        P("phase", "dp", None, None),
        P("phase", "dp", None, None),
        P("phase", "dp", None, None),
        P("phase", "dp", None, None),
        P("phase", "dp", None, None),
        P("phase", "dp", None, None),
        P("phase", None),
        P("phase", "dp", None),
        P("phase", "dp", None),
        P(),
        P(),
        P(),
        P(),
        P(),
        P("dp"),
        P("dp", None),
    )
    return jax.shard_map(
        shards,
        mesh=mesh,
        in_specs=placed,
        out_specs=(
            P("phase", "dp", None, None),
            P("phase", "dp", None, None),
            P("phase", "dp", None, None),
            P("phase", "dp", None, None),
        ),
        check_vma=False,
    )
```

```python
import functools
import math

import jax
import jax.numpy as jnp
from jax import lax
from jax.experimental import pallas as pl
from jax.experimental.pallas import tpu as pltpu
from jax.sharding import PartitionSpec as P

HEAD_DIM = 128
TICKS = 3
WINDOW = 64
TILE = 16
GRANT = 12 * 1024 * 1024

epsilon = 1e-06

X, Y, C = 2, 4, 2


def spot(x, y, core):
    return ((x % X) * Y + (y % Y)) * C + core


def moved(value, dx, dy, dc):
    pairs = [
        (spot(x, y, c), spot(x + dx, y + dy, (c + dc) % C))
        for x in range(X)
        for y in range(Y)
        for c in range(C)
    ]
    return lax.ppermute(value, "dp", pairs)


def shifted(value):
    count = lax.axis_size("phase")
    pairs = [(source, (source + 1) % count) for source in range(count)]
    return lax.ppermute(value, "phase", pairs)


def joined(*values):
    return lax.optimization_barrier(values)


NEAR = [
    (0, 0, 0, 16),
    (0, -1, 0, 8),
    (0, -1, 8, 8),
    (0, 1, 0, 8),
    (0, 1, 8, 8),
    (1, 0, 0, 8),
    (1, 0, 8, 8),
]
MIDDLE = [(0, 2, 0, 8), (0, 2, 8, 8), (1, -1, 0, 8), (1, 1, 0, 8), (1, 2, 0, 8)]
LAST = [(1, -1, 8, 8), (1, 1, 8, 8), (1, 2, 8, 8)]


def in_hbm(array):
    return pltpu.with_memory_space_constraint(array, pltpu.HBM)


def pair(piece):
    return moved(piece, 0, 0, 1)


def places(rows, group):
    device = lax.axis_index("dp")
    core = lax.rem(device, C)
    y = lax.rem(device // C, Y)
    x = device // (C * Y)
    found = []
    for dx, dy, dc, part, count in group:
        source = (lax.rem(x + dx, X) * Y + lax.rem(y + dy + Y, Y)) * C + lax.rem(core + dc, C)
        found.append((pl.multiple_of(source * rows + part * rows // 16, TILE), count * rows // 16))
    return found


def both(group):
    return [(dx, dy, dc, part, count) for dc in range(C) for dx, dy, part, count in group]


def normalize(widened):
    return widened * lax.rsqrt(jnp.mean(widened * widened, axis=-1, keepdims=True) + epsilon)


def batch_of(tick, section, sections, lengths_ref):
    patches = lengths_ref.shape[1]
    slot = lax.rem(tick - section + sections, sections)
    picture = slot // patches
    segment = lax.rem(slot, patches)
    length = lengths_ref[picture, segment]
    offset = jnp.int32(0)
    for m in range(patches - 1):
        offset = offset + jnp.where(m < segment, lengths_ref[picture, m], 0)
    return picture, length, offset


def embedded_rows(latents, embed_w_ref, embed_b_ref, live):
    rows = jnp.dot(latents, embed_w_ref[...], preferred_element_type=jnp.float32) + embed_b_ref[...][None]
    row_ids = lax.broadcasted_iota(jnp.int32, rows.shape, 0)
    return jnp.where(row_ids < live, rows, 0.0).astype(jnp.bfloat16)


def attend(proj, image_k, image_v, text_k, text_v, attended):
    width = attended.shape[1]
    scale = 1.0 / math.sqrt(HEAD_DIM)
    across = (((1,), (1,)), ((), ()))
    for head in range(width // HEAD_DIM):
        cols = slice(head * HEAD_DIM, (head + 1) * HEAD_DIM)
        queries = proj[:, cols]
        on_text = lax.dot_general(queries, text_k[:, cols], across, preferred_element_type=jnp.float32)
        on_image = lax.dot_general(queries, image_k[:, cols], across, preferred_element_type=jnp.float32)
        highest = jnp.maximum(
            jnp.max(on_text, axis=-1, keepdims=True), jnp.max(on_image, axis=-1, keepdims=True)
        )
        on_text = jnp.exp((on_text - highest) * scale)
        on_image = jnp.exp((on_image - highest) * scale)
        total = jnp.sum(on_text, axis=-1, keepdims=True) + jnp.sum(on_image, axis=-1, keepdims=True)
        mixed = jnp.dot(
            on_text.astype(jnp.bfloat16), text_v[:, cols], preferred_element_type=jnp.float32
        ) + jnp.dot(on_image.astype(jnp.bfloat16), image_v[:, cols], preferred_element_type=jnp.float32)
        attended[:, cols] = (mixed / total).astype(jnp.bfloat16)


def weight_copies(pieces, weights, rows, group, sems):
    return [
        pltpu.make_async_copy(piece, weights.at[pl.ds(start, count), :], sems.at[at])
        for at, (piece, (start, count)) in enumerate(zip(pieces, places(rows, group)))
    ]


def run_copies(copies):
    for copy in copies:
        copy.start()
    for copy in copies:
        copy.wait()


def own_kernel(qkv, out, low, high, whole, sems):
    half, width = low.shape[0], qkv.shape[1]
    copies = []
    for at, (target, start) in enumerate(((low, 0), (high, half), (whole, 0))):
        rows = pl.ds(start, target.shape[0])
        copies += [
            pltpu.make_async_copy(qkv.at[rows, :], target.at[:, pl.ds(0, width)], sems.at[2 * at]),
            pltpu.make_async_copy(
                out.at[rows, :], target.at[:, pl.ds(width, out.shape[1])], sems.at[2 * at + 1]
            ),
        ]
    run_copies(copies)


def load_kernel(rows, group, copied, first, *refs):
    if not first:
        refs = refs[1:]
    count = len(group)
    pieces, sources, refs = refs[:count], refs[count : count + copied], refs[count + copied :]
    weights, targets, (sems, copy_sems, *stages) = refs[0], refs[1 : 1 + copied], refs[1 + copied :]
    inward = [
        pltpu.make_async_copy(source, stage, copy_sems.at[at, 0])
        for at, (source, stage) in enumerate(zip(sources, stages))
    ]
    outward = [
        pltpu.make_async_copy(stage, target, copy_sems.at[at, 1])
        for at, (stage, target) in enumerate(zip(stages, targets))
    ]
    copies = weight_copies(pieces, weights, rows, group, sems)
    for copy in inward + copies:
        copy.start()
    for copy, onward in zip(inward, outward):
        copy.wait()
        onward.start()
    for copy in copies + outward:
        copy.wait()


def tick_kernel(tick, sections, first, rows, *refs):
    lengths, steps, sigmas = refs[:3]
    gain, embed_w, embed_b, head_w, head_b = refs[3:8]
    text_k, text_v, keys_in, values_in = refs[8:12]
    rest = refs[12:]
    if first:
        hidden_in, latents_in, _ = rest[:3]
        pieces = rest[3 : 3 + C * len(LAST)]
        keys, values, weights, sent, *scratch = rest[3 + C * len(LAST) :]
    else:
        received, weights = rest[:2]
        keys, values, sent, *scratch = rest[2:]
    hidden, image_k, image_v, txt_k, txt_v, proj, attended, cache_sem, back_sem, *weight_sem = scratch
    width = hidden.shape[1]
    section = lax.axis_index("phase")
    picture, length, offset = batch_of(tick, section, sections, lengths)
    base = pl.multiple_of(jnp.minimum((offset // TILE) * TILE, image_k.shape[0] - WINDOW), TILE)

    loads = [
        pltpu.make_async_copy(source.at[picture], target, cache_sem.at[at])
        for at, (source, target) in enumerate(
            [(keys_in, image_k), (values_in, image_v), (text_k, txt_k), (text_v, txt_v)]
        )
    ]
    weight_loads = []
    if first:
        weight_loads = weight_copies(pieces, weights, rows, both(LAST), weight_sem[0])
    for load in weight_loads + loads:
        load.start()

    if first:
        hidden[...] = hidden_in[...]
    else:
        hidden[...] = received[:, :width]

        @pl.when(section == 0)
        def _():
            hidden[...] = embedded_rows(
                received[:, width : width + embed_w.shape[0]], embed_w, embed_b, lengths[0, tick]
            )

    normed = (normalize(hidden[...].astype(jnp.float32)) * gain[...]).astype(jnp.bfloat16)
    for load in weight_loads:
        load.wait()
    for block in range(3):
        cols = slice(block * width, (block + 1) * width)
        proj[:, cols] = jnp.dot(normed, weights[:, cols], preferred_element_type=jnp.float32).astype(
            jnp.bfloat16
        )
    for load in loads:
        load.wait()

    token = lax.broadcasted_iota(jnp.int32, (WINDOW, proj.shape[0]), 0) + base - offset
    place = (token == lax.broadcasted_iota(jnp.int32, token.shape, 1)) & (token < length)
    place = place.astype(jnp.bfloat16)
    token = lax.broadcasted_iota(jnp.int32, (WINDOW, width), 0) + base - offset
    inside = (token >= 0) & (token < length)
    for block, cache in ((1, image_k), (2, image_v)):
        fresh = jnp.dot(
            place, proj[:, block * width : (block + 1) * width], preferred_element_type=jnp.float32
        )
        old = cache[pl.ds(base, WINDOW), :].astype(jnp.float32)
        cache[pl.ds(base, WINDOW), :] = jnp.where(inside, fresh, old).astype(jnp.bfloat16)
    backs = [
        pltpu.make_async_copy(
            source.at[pl.ds(base, WINDOW), :],
            target.at[picture, pl.ds(base, WINDOW), :],
            back_sem.at[at],
        )
        for at, (source, target) in enumerate([(image_k, keys), (image_v, values)])
    ]
    for back in backs:
        back.start()

    attend(proj, image_k, image_v, txt_k, txt_v, attended)

    summed = hidden[...].astype(jnp.float32) + jnp.dot(
        attended[...], weights[:, 3 * width :], preferred_element_type=jnp.float32
    )
    row_ids = lax.broadcasted_iota(jnp.int32, summed.shape, 0)
    hidden_new = jnp.where(row_ids < length, summed, 0.0).astype(jnp.bfloat16)
    sent[:, :width] = hidden_new
    channels = embed_w.shape[0]
    latents = latents_in[...] if first else received[:, width : width + channels]
    sent[:, width:] = jnp.concatenate(
        [latents, jnp.zeros((latents.shape[0], sent.shape[1] - width - channels), latents.dtype)], axis=1
    )

    @pl.when(section == sections - 1)
    def _():
        velocity = (
            lax.dot_general(
                normalize(hidden_new.astype(jnp.float32)).astype(jnp.bfloat16),
                head_w[...],
                (((1,), (1,)), ((), ())),
                preferred_element_type=jnp.float32,
            )
            + head_b[...][None]
        )
        step = steps[picture]
        jump = sigmas[step + 1] - sigmas[step]
        stepped = latents.astype(jnp.float32) + jump * velocity
        row_ids = lax.broadcasted_iota(jnp.int32, stepped.shape, 0)
        stepped = jnp.where(row_ids < length, stepped, 0.0).astype(jnp.bfloat16)
        sent[:, width:] = jnp.concatenate(
            [stepped, jnp.zeros((latents.shape[0], sent.shape[1] - width - channels), latents.dtype)],
            axis=1,
        )

    for back in backs:
        back.wait()


def final_kernel(tick, lengths, embed_w, embed_b, received, hidden, latents):
    width = hidden.shape[1]
    arrived = received[:, width : width + latents.shape[1]]
    hidden[...] = received[:, :width]
    latents[...] = arrived

    @pl.when(lax.axis_index("phase") == 0)
    def _():
        hidden[...] = embedded_rows(arrived, embed_w, embed_b, lengths[0, tick])


def shards(
    hidden_flight,
    latent_flight,
    key_cache,
    value_cache,
    text_keys,
    text_values,
    norm_gain,
    w_qkv,
    w_out,
    embed_weight,
    embed_bias,
    head_weight,
    head_bias,
    sigma_table,
    step_index,
    patch_lengths,
):
    sections = lax.axis_size("phase")
    hidden = hidden_flight[0, 0]
    latents = latent_flight[0, 0]
    keys, values = key_cache[0], value_cache[0]
    rows, width = hidden.shape
    wide = width + HEAD_DIM
    tokens = keys.shape[1]
    part = w_qkv.shape[1]
    full = part * lax.axis_size("dp")
    smem = pl.BlockSpec(memory_space=pltpu.SMEM)
    vmem = pl.BlockSpec(memory_space=pltpu.VMEM)
    hbm = pl.BlockSpec(memory_space=pl.ANY)
    scalars = [patch_lengths, step_index, sigma_table]
    small = [norm_gain, embed_weight, embed_bias, head_weight.T, head_bias]
    texts = [text_keys[0], text_values[0]]
    params = pltpu.CompilerParams(vmem_limit_bytes=GRANT)
    small_params = pltpu.CompilerParams(vmem_limit_bytes=GRANT // 2)

    full = part * lax.axis_size("dp")
    total = w_qkv.shape[2] + w_out.shape[2]
    halves = [jax.ShapeDtypeStruct((part // 2, total), jnp.bfloat16)] * 2
    low, high, whole = pl.pallas_call(
        own_kernel,
        out_shape=halves + [jax.ShapeDtypeStruct((part, total), jnp.bfloat16)],
        in_specs=[hbm] * 2,
        out_specs=[hbm] * 3,
        scratch_shapes=[pltpu.SemaphoreType.DMA((6,))],
        compiler_params=small_params,
        name="own",
    )(in_hbm(w_qkv[0]), in_hbm(w_out[0]))

    def loaded(weights, pieces, group, copied, name):
        first = weights is None
        if not first:
            weights = pltpu.with_memory_space_constraint(weights, pltpu.VMEM)
        return pl.pallas_call(
            functools.partial(load_kernel, part, group, len(copied), first),
            out_shape=[pltpu.VMEM((full, total), jnp.bfloat16)]
            + [jax.ShapeDtypeStruct(array.shape, array.dtype) for array in copied],
            in_specs=[vmem] * (not first) + [hbm] * (len(pieces) + len(copied)),
            out_specs=[vmem] + [hbm] * len(copied),
            scratch_shapes=[
                pltpu.SemaphoreType.DMA((len(pieces),)),
                pltpu.SemaphoreType.DMA((max(len(copied), 1), 2)),
                *[pltpu.VMEM(array.shape, array.dtype) for array in copied],
            ],
            input_output_aliases={} if first else {0: 0},
            compiler_params=small_params,
            name=name,
        )(*([] if first else [weights]), *pieces, *[in_hbm(array) for array in copied])

    below_low, above_high, across_low = moved(low, 0, 1, 0), moved(high, 0, -1, 0), moved(low, 1, 0, 0)
    below_high, above_low = moved(high, 0, 1, 0), moved(low, 0, -1, 0)
    far_low, far_high = moved(below_low, 0, 1, 0), moved(above_high, 0, -1, 0)
    across_high = moved(joined(high, across_low)[0], 1, 0, 0)
    ready = joined(whole, below_low, above_high, across_low, below_high, below_high, above_low, across_high)
    whole_pair, below_low_pair, above_high_pair, across_low_pair, below_high_pair = [pair(piece) for piece in ready[:5]]
    far_low, far_high, onward_low, onward_high, *ready = joined(
        far_low, far_high, across_low, across_high, above_low, across_high, whole_pair, below_low_pair, above_high_pair, across_low_pair, below_high_pair
    )
    above_low_pair, across_high_pair = [pair(piece) for piece in ready[:2]]
    xu_low, xd_low, xf_low = moved(onward_low, 0, 1, 0), moved(onward_low, 0, -1, 0), moved(far_low, 1, 0, 0)
    xu_high, xd_high, xf_high = moved(onward_high, 0, 1, 0), moved(onward_high, 0, -1, 0), moved(far_high, 1, 0, 0)
    near = [whole, below_low, below_high, above_low, above_high, across_low, across_high]
    near += [whole_pair, below_low_pair, below_high_pair, above_low_pair, above_high_pair, across_low_pair, across_high_pair]
    weights, keys, values = loaded(None, near, both(NEAR), [keys, values], "near")
    low_set = [far_low, far_high, xu_low, xd_low, xf_low]
    keys, *low_set = joined(keys, *low_set)
    middle = low_set + [pair(piece) for piece in low_set]
    weights, latents = loaded(weights, middle, both(MIDDLE), [latents], "middle")
    latents, *last = joined(latents, xu_high, xd_high, xf_high)
    last += [pair(piece) for piece in last]

    for tick in range(TICKS):
        first = tick == 0
        weights = pltpu.with_memory_space_constraint(weights, pltpu.VMEM)
        if first:
            own = [hidden, latents, weights] + last
            own_specs = [vmem] * 3 + [hbm] * len(last)
        else:
            own = [received, weights]
            own_specs = [vmem] * 2
        shapes = [
            jax.ShapeDtypeStruct(keys.shape, keys.dtype),
            jax.ShapeDtypeStruct(values.shape, values.dtype),
        ]
        out_specs = [hbm, hbm]
        aliases = {10: 0, 11: 1}
        if first:
            shapes.append(pltpu.VMEM(weights.shape, weights.dtype))
            out_specs.append(vmem)
            aliases[14] = 2
        shapes.append(jax.ShapeDtypeStruct((rows, wide), jnp.bfloat16))
        out_specs.append(vmem)
        scratch = [
            pltpu.VMEM((rows, width), jnp.bfloat16),
            *[pltpu.VMEM((tokens, width), jnp.bfloat16)] * 4,
            pltpu.VMEM((rows, 3 * width), jnp.bfloat16),
            pltpu.VMEM((rows, width), jnp.bfloat16),
            pltpu.SemaphoreType.DMA((4,)),
            pltpu.SemaphoreType.DMA((2,)),
        ]
        if first:
            scratch.append(pltpu.SemaphoreType.DMA((len(last),)))
        results = pl.pallas_call(
            functools.partial(tick_kernel, tick, sections, first, part),
            out_shape=shapes,
            in_specs=[smem] * 3 + [vmem] * 5 + [hbm] * 4 + own_specs,
            out_specs=out_specs,
            scratch_shapes=scratch,
            input_output_aliases=aliases,
            compiler_params=params,
            name=f"tick{tick}",
        )(*scalars, *small, *texts, keys, values, *own)
        if first:
            keys, values, weights, sent = results
        else:
            keys, values, sent = results
        received = shifted(sent)

    hidden, latents = pl.pallas_call(
        functools.partial(final_kernel, TICKS),
        out_shape=[
            jax.ShapeDtypeStruct(hidden.shape, hidden.dtype),
            jax.ShapeDtypeStruct(latents.shape, latents.dtype),
        ],
        in_specs=[smem, vmem, vmem, vmem],
        out_specs=[vmem, vmem],
        compiler_params=params,
        name="final",
    )(patch_lengths, embed_weight, embed_bias, received)
    return (hidden[None, None], latents[None, None], keys[None], values[None])


def solution(mesh):
    placed = (
        P("phase", "dp", None, None),
        P("phase", "dp", None, None),
        P("phase", "dp", None, None),
        P("phase", "dp", None, None),
        P("phase", "dp", None, None),
        P("phase", "dp", None, None),
        P("phase", None),
        P("phase", "dp", None),
        P("phase", "dp", None),
        P(),
        P(),
        P(),
        P(),
        P(),
        P("dp"),
        P("dp", None),
    )
    return jax.shard_map(
        shards,
        mesh=mesh,
        in_specs=placed,
        out_specs=(
            P("phase", "dp", None, None),
            P("phase", "dp", None, None),
            P("phase", "dp", None, None),
            P("phase", "dp", None, None),
        ),
        check_vma=False,
    )
```

```python
import functools
import math

import jax
import jax.numpy as jnp
from jax import lax
from jax.experimental import pallas as pl
from jax.experimental.pallas import tpu as pltpu
from jax.sharding import PartitionSpec as P

HEAD_DIM = 128
TICKS = 3
WINDOW = 64
TILE = 16
GRANT = 12 * 1024 * 1024

epsilon = 1e-06

X, Y, C = 2, 4, 2


def spot(x, y, core):
    return ((x % X) * Y + (y % Y)) * C + core


def moved(value, dx, dy, dc):
    pairs = [
        (spot(x, y, c), spot(x + dx, y + dy, (c + dc) % C))
        for x in range(X)
        for y in range(Y)
        for c in range(C)
    ]
    return lax.ppermute(value, "dp", pairs)


def shifted(value):
    count = lax.axis_size("phase")
    pairs = [(source, (source + 1) % count) for source in range(count)]
    return lax.ppermute(value, "phase", pairs)


def joined(*values):
    return lax.optimization_barrier(values)


LOW, HIGH = 0, 1
NEAR = [
    [(0, 0, 0, LOW)],
    [(0, 0, 0, HIGH)],
    [(0, -1, 0, LOW)],
    [(0, 1, 0, HIGH)],
    [(1, 0, 0, LOW)],
    [(1, 0, 0, HIGH)],
    [(0, 2, 0, LOW)],
    [(0, 2, 0, HIGH)],
]
FAR = [[(1, 2, 0, LOW), (1, 2, 0, HIGH)]]
LAST = [
    [(0, -1, 0, HIGH), (1, -1, 0, LOW), (1, -1, 0, HIGH)],
    [(0, 1, 0, LOW), (1, 1, 0, LOW), (1, 1, 0, HIGH)],
]


def paired(pieces):
    return [[(dx, dy, 1, half) for dx, dy, _, half in piece] for piece in pieces]


def in_hbm(array):
    return pltpu.with_memory_space_constraint(array, pltpu.HBM)


def pair(piece):
    return moved(piece, 0, 0, 1)


def place(rows, block):
    dx, dy, dc, half = block
    device = lax.axis_index("dp")
    core = lax.rem(device % C + dc, C)
    y = lax.rem((device // C) % Y + dy + Y, Y)
    x = lax.rem(device // (C * Y) + dx, X)
    return pl.multiple_of(((x * Y + y) * C + core) * rows + half * (rows // 2), TILE)


def normalize(widened):
    return widened * lax.rsqrt(jnp.mean(widened * widened, axis=-1, keepdims=True) + epsilon)


def batch_of(tick, section, sections, lengths_ref):
    patches = lengths_ref.shape[1]
    slot = lax.rem(tick - section + sections, sections)
    picture = slot // patches
    segment = lax.rem(slot, patches)
    length = lengths_ref[picture, segment]
    offset = jnp.int32(0)
    for m in range(patches - 1):
        offset = offset + jnp.where(m < segment, lengths_ref[picture, m], 0)
    return picture, length, offset


def embedded_rows(latents, embed_w_ref, embed_b_ref, live):
    rows = jnp.dot(latents, embed_w_ref[...], preferred_element_type=jnp.float32) + embed_b_ref[...][None]
    row_ids = lax.broadcasted_iota(jnp.int32, rows.shape, 0)
    return jnp.where(row_ids < live, rows, 0.0).astype(jnp.bfloat16)


def attend(proj, image_k, image_v, text_k, text_v, attended):
    width = attended.shape[1]
    scale = 1.0 / math.sqrt(HEAD_DIM)
    across = (((1,), (1,)), ((), ()))
    for head in range(width // HEAD_DIM):
        cols = slice(head * HEAD_DIM, (head + 1) * HEAD_DIM)
        queries = proj[:, cols]
        on_text = lax.dot_general(queries, text_k[:, cols], across, preferred_element_type=jnp.float32)
        on_image = lax.dot_general(queries, image_k[:, cols], across, preferred_element_type=jnp.float32)
        highest = jnp.maximum(
            jnp.max(on_text, axis=-1, keepdims=True), jnp.max(on_image, axis=-1, keepdims=True)
        )
        on_text = jnp.exp((on_text - highest) * scale)
        on_image = jnp.exp((on_image - highest) * scale)
        total = jnp.sum(on_text, axis=-1, keepdims=True) + jnp.sum(on_image, axis=-1, keepdims=True)
        mixed = jnp.dot(
            on_text.astype(jnp.bfloat16), text_v[:, cols], preferred_element_type=jnp.float32
        ) + jnp.dot(on_image.astype(jnp.bfloat16), image_v[:, cols], preferred_element_type=jnp.float32)
        attended[:, cols] = (mixed / total).astype(jnp.bfloat16)


def weight_copies(pieces, weights, rows, blocks, sems):
    size = rows // 2
    found = []
    for piece, held in zip(pieces, blocks):
        for at, block in enumerate(held):
            found.append(
                pltpu.make_async_copy(
                    piece.at[pl.ds(at * size, size), :],
                    weights.at[pl.ds(place(rows, block), size), :],
                    sems.at[len(found)],
                )
            )
    return found


def run_copies(copies):
    for copy in copies:
        copy.start()
    for copy in copies:
        copy.wait()


def own_kernel(qkv, out, low, high, sems):
    half, width = low.shape[0], qkv.shape[1]
    copies = []
    for at, target in enumerate((low, high)):
        rows = pl.ds(at * half, half)
        copies += [
            pltpu.make_async_copy(qkv.at[rows, :], target.at[:, pl.ds(0, width)], sems.at[2 * at]),
            pltpu.make_async_copy(
                out.at[rows, :], target.at[:, pl.ds(width, out.shape[1])], sems.at[2 * at + 1]
            ),
        ]
    run_copies(copies)


def stack_kernel(stacks, count, *refs):
    pieces, targets, sems = refs[:count], refs[count:-1], refs[-1]
    size = pieces[0].shape[0]
    copies = []
    for target, held in zip(targets, stacks):
        for at, piece in enumerate(held):
            copies.append(
                pltpu.make_async_copy(
                    pieces[piece], target.at[pl.ds(at * size, size), :], sems.at[len(copies)]
                )
            )
    run_copies(copies)


def load_kernel(rows, first, blocks, count, copied, *refs):
    if not first:
        refs = refs[1:]
    pieces, sources, refs = refs[:count], refs[count : count + copied], refs[count + copied :]
    weights, targets, refs = refs[0], refs[1 : 1 + copied], refs[1 + copied :]
    sems, copy_sems, stages = refs[0], refs[1], refs[2:]
    copies = weight_copies(pieces, weights, rows, blocks, sems)
    inward = [
        pltpu.make_async_copy(source, stage, copy_sems.at[at, 0])
        for at, (source, stage) in enumerate(zip(sources, stages))
    ]
    outward = [
        pltpu.make_async_copy(stage, target, copy_sems.at[at, 1])
        for at, (stage, target) in enumerate(zip(stages, targets))
    ]
    for copy in inward + copies:
        copy.start()
    for copy, onward in zip(inward, outward):
        copy.wait()
        onward.start()
    for copy in copies + outward:
        copy.wait()


def tick_kernel(tick, sections, first, rows, *refs):
    lengths, steps, sigmas = refs[:3]
    gain, embed_w, embed_b, head_w, head_b = refs[3:8]
    text_k, text_v, keys_in, values_in = refs[8:12]
    rest = refs[12:]
    if first:
        hidden_in, latents_in, _ = rest[:3]
        pieces = rest[3 : 3 + C * len(LAST)]
        keys, values, weights, sent, *scratch = rest[3 + C * len(LAST) :]
    else:
        received, weights = rest[:2]
        keys, values, sent, *scratch = rest[2:]
    hidden, image_k, image_v, txt_k, txt_v, proj, attended, cache_sem, back_sem, *weight_sem = scratch
    width = hidden.shape[1]
    section = lax.axis_index("phase")
    picture, length, offset = batch_of(tick, section, sections, lengths)
    base = pl.multiple_of(jnp.minimum((offset // TILE) * TILE, image_k.shape[0] - WINDOW), TILE)

    loads = [
        pltpu.make_async_copy(source.at[picture], target, cache_sem.at[at])
        for at, (source, target) in enumerate(
            [(keys_in, image_k), (values_in, image_v), (text_k, txt_k), (text_v, txt_v)]
        )
    ]
    weight_loads = []
    if first:
        weight_loads = weight_copies(pieces, weights, rows, LAST + paired(LAST), weight_sem[0])
    for load in weight_loads + loads:
        load.start()

    if first:
        hidden[...] = hidden_in[...]
    else:
        hidden[...] = received[:, :width]

        @pl.when(section == 0)
        def _():
            hidden[...] = embedded_rows(
                received[:, width : width + embed_w.shape[0]], embed_w, embed_b, lengths[0, tick]
            )

    normed = (normalize(hidden[...].astype(jnp.float32)) * gain[...]).astype(jnp.bfloat16)
    for load in weight_loads:
        load.wait()
    for block in range(3):
        cols = slice(block * width, (block + 1) * width)
        proj[:, cols] = jnp.dot(normed, weights[:, cols], preferred_element_type=jnp.float32).astype(
            jnp.bfloat16
        )
    for load in loads:
        load.wait()

    token = lax.broadcasted_iota(jnp.int32, (WINDOW, proj.shape[0]), 0) + base - offset
    place = (token == lax.broadcasted_iota(jnp.int32, token.shape, 1)) & (token < length)
    place = place.astype(jnp.bfloat16)
    token = lax.broadcasted_iota(jnp.int32, (WINDOW, width), 0) + base - offset
    inside = (token >= 0) & (token < length)
    for block, cache in ((1, image_k), (2, image_v)):
        fresh = jnp.dot(
            place, proj[:, block * width : (block + 1) * width], preferred_element_type=jnp.float32
        )
        old = cache[pl.ds(base, WINDOW), :].astype(jnp.float32)
        cache[pl.ds(base, WINDOW), :] = jnp.where(inside, fresh, old).astype(jnp.bfloat16)
    backs = [
        pltpu.make_async_copy(
            source.at[pl.ds(base, WINDOW), :],
            target.at[picture, pl.ds(base, WINDOW), :],
            back_sem.at[at],
        )
        for at, (source, target) in enumerate([(image_k, keys), (image_v, values)])
    ]
    for back in backs:
        back.start()

    attend(proj, image_k, image_v, txt_k, txt_v, attended)

    summed = hidden[...].astype(jnp.float32) + jnp.dot(
        attended[...], weights[:, 3 * width :], preferred_element_type=jnp.float32
    )
    row_ids = lax.broadcasted_iota(jnp.int32, summed.shape, 0)
    hidden_new = jnp.where(row_ids < length, summed, 0.0).astype(jnp.bfloat16)
    sent[:, :width] = hidden_new
    channels = embed_w.shape[0]
    latents = latents_in[...] if first else received[:, width : width + channels]
    sent[:, width:] = jnp.concatenate(
        [latents, jnp.zeros((latents.shape[0], sent.shape[1] - width - channels), latents.dtype)], axis=1
    )

    @pl.when(section == sections - 1)
    def _():
        velocity = (
            lax.dot_general(
                normalize(hidden_new.astype(jnp.float32)).astype(jnp.bfloat16),
                head_w[...],
                (((1,), (1,)), ((), ())),
                preferred_element_type=jnp.float32,
            )
            + head_b[...][None]
        )
        step = steps[picture]
        jump = sigmas[step + 1] - sigmas[step]
        stepped = latents.astype(jnp.float32) + jump * velocity
        row_ids = lax.broadcasted_iota(jnp.int32, stepped.shape, 0)
        stepped = jnp.where(row_ids < length, stepped, 0.0).astype(jnp.bfloat16)
        sent[:, width:] = jnp.concatenate(
            [stepped, jnp.zeros((latents.shape[0], sent.shape[1] - width - channels), latents.dtype)],
            axis=1,
        )

    for back in backs:
        back.wait()


def final_kernel(tick, lengths, embed_w, embed_b, received, hidden, latents):
    width = hidden.shape[1]
    arrived = received[:, width : width + latents.shape[1]]
    hidden[...] = received[:, :width]
    latents[...] = arrived

    @pl.when(lax.axis_index("phase") == 0)
    def _():
        hidden[...] = embedded_rows(arrived, embed_w, embed_b, lengths[0, tick])


def shards(
    hidden_flight,
    latent_flight,
    key_cache,
    value_cache,
    text_keys,
    text_values,
    norm_gain,
    w_qkv,
    w_out,
    embed_weight,
    embed_bias,
    head_weight,
    head_bias,
    sigma_table,
    step_index,
    patch_lengths,
):
    sections = lax.axis_size("phase")
    hidden = hidden_flight[0, 0]
    latents = latent_flight[0, 0]
    keys, values = key_cache[0], value_cache[0]
    rows, width = hidden.shape
    wide = width + HEAD_DIM
    tokens = keys.shape[1]
    part = w_qkv.shape[1]
    full = part * lax.axis_size("dp")
    smem = pl.BlockSpec(memory_space=pltpu.SMEM)
    vmem = pl.BlockSpec(memory_space=pltpu.VMEM)
    hbm = pl.BlockSpec(memory_space=pl.ANY)
    scalars = [patch_lengths, step_index, sigma_table]
    small = [norm_gain, embed_weight, embed_bias, head_weight.T, head_bias]
    texts = [text_keys[0], text_values[0]]
    params = pltpu.CompilerParams(vmem_limit_bytes=GRANT)
    small_params = pltpu.CompilerParams(vmem_limit_bytes=GRANT // 2)

    full = part * lax.axis_size("dp")
    total = w_qkv.shape[2] + w_out.shape[2]
    half = jax.ShapeDtypeStruct((part // 2, total), jnp.bfloat16)
    low, high = pl.pallas_call(
        own_kernel,
        out_shape=[half] * 2,
        in_specs=[hbm] * 2,
        out_specs=[hbm] * 2,
        scratch_shapes=[pltpu.SemaphoreType.DMA((4,))],
        compiler_params=small_params,
        name="own",
    )(in_hbm(w_qkv[0]), in_hbm(w_out[0]))

    def stacked(pieces, stacks):
        return pl.pallas_call(
            functools.partial(stack_kernel, stacks, len(pieces)),
            out_shape=[
                jax.ShapeDtypeStruct((len(held) * (part // 2), total), jnp.bfloat16) for held in stacks
            ],
            in_specs=[hbm] * len(pieces),
            out_specs=[hbm] * len(stacks),
            scratch_shapes=[pltpu.SemaphoreType.DMA((sum(len(held) for held in stacks),))],
            compiler_params=small_params,
            name="stack",
        )(*pieces)

    def loaded(name, weights, pieces, blocks, copied):
        first = weights is None
        if not first:
            weights = pltpu.with_memory_space_constraint(weights, pltpu.VMEM)
        shapes = [pltpu.VMEM((full, total), jnp.bfloat16)]
        shapes += [jax.ShapeDtypeStruct(array.shape, array.dtype) for array in copied]
        return pl.pallas_call(
            functools.partial(load_kernel, part, first, blocks, len(pieces), len(copied)),
            out_shape=shapes,
            in_specs=[vmem] * (not first) + [hbm] * (len(pieces) + len(copied)),
            out_specs=[vmem] + [hbm] * (len(shapes) - 1),
            scratch_shapes=[
                pltpu.SemaphoreType.DMA((sum(len(held) for held in blocks),)),
                pltpu.SemaphoreType.DMA((len(copied), 2)),
                *[pltpu.VMEM(array.shape, array.dtype) for array in copied],
            ],
            input_output_aliases={} if first else {0: 0},
            compiler_params=small_params,
            name=name,
        )(*([] if first else [weights]), *pieces, *[in_hbm(array) for array in copied])

    below_low, above_high = moved(low, 0, 1, 0), moved(high, 0, -1, 0)
    across_low, across_high = moved(low, 1, 0, 0), moved(high, 1, 0, 0)
    far_low, far_high = moved(below_low, 0, 1, 0), moved(above_high, 0, -1, 0)
    near = [low, high, below_low, above_high, across_low, across_high, far_low, far_high]
    near_pair, up, down, far = stacked(near, [list(range(8)), [1, 4, 5], [0, 4, 5], [6, 7]])
    near_pair = pair(near_pair)
    up, down, far = moved(up, 0, 1, 0), moved(down, 0, -1, 0), moved(far, 1, 0, 0)
    weights, keys, values = loaded(
        "near",
        None,
        [*near, near_pair],
        NEAR + [[block for piece in paired(NEAR) for block in piece]],
        [keys, values],
    )
    keys, far = joined(keys, far)
    far_pair = pair(far)
    up, down, far_pair = joined(up, down, far_pair)
    weights, latents = loaded("far", weights, [far, far_pair], FAR + paired(FAR), [latents])
    last = [up, down]
    last += [pair(piece) for piece in last]

    for tick in range(TICKS):
        first = tick == 0
        weights = pltpu.with_memory_space_constraint(weights, pltpu.VMEM)
        if first:
            own = [hidden, latents, weights] + last
            own_specs = [vmem] * 3 + [hbm] * len(last)
        else:
            own = [received, weights]
            own_specs = [vmem] * 2
        shapes = [
            jax.ShapeDtypeStruct(keys.shape, keys.dtype),
            jax.ShapeDtypeStruct(values.shape, values.dtype),
        ]
        out_specs = [hbm, hbm]
        aliases = {10: 0, 11: 1}
        if first:
            shapes.append(pltpu.VMEM(weights.shape, weights.dtype))
            out_specs.append(vmem)
            aliases[14] = 2
        shapes.append(jax.ShapeDtypeStruct((rows, wide), jnp.bfloat16))
        out_specs.append(vmem)
        scratch = [
            pltpu.VMEM((rows, width), jnp.bfloat16),
            *[pltpu.VMEM((tokens, width), jnp.bfloat16)] * 4,
            pltpu.VMEM((rows, 3 * width), jnp.bfloat16),
            pltpu.VMEM((rows, width), jnp.bfloat16),
            pltpu.SemaphoreType.DMA((4,)),
            pltpu.SemaphoreType.DMA((2,)),
        ]
        if first:
            scratch.append(pltpu.SemaphoreType.DMA((2 * sum(len(held) for held in LAST),)))
        results = pl.pallas_call(
            functools.partial(tick_kernel, tick, sections, first, part),
            out_shape=shapes,
            in_specs=[smem] * 3 + [vmem] * 5 + [hbm] * 4 + own_specs,
            out_specs=out_specs,
            scratch_shapes=scratch,
            input_output_aliases=aliases,
            compiler_params=params,
            name=f"tick{tick}",
        )(*scalars, *small, *texts, keys, values, *own)
        if first:
            keys, values, weights, sent = results
        else:
            keys, values, sent = results
        received = shifted(sent)

    hidden, latents = pl.pallas_call(
        functools.partial(final_kernel, TICKS),
        out_shape=[
            jax.ShapeDtypeStruct(hidden.shape, hidden.dtype),
            jax.ShapeDtypeStruct(latents.shape, latents.dtype),
        ],
        in_specs=[smem, vmem, vmem, vmem],
        out_specs=[vmem, vmem],
        compiler_params=params,
        name="final",
    )(patch_lengths, embed_weight, embed_bias, received)
    return (hidden[None, None], latents[None, None], keys[None], values[None])


def solution(mesh):
    placed = (
        P("phase", "dp", None, None),
        P("phase", "dp", None, None),
        P("phase", "dp", None, None),
        P("phase", "dp", None, None),
        P("phase", "dp", None, None),
        P("phase", "dp", None, None),
        P("phase", None),
        P("phase", "dp", None),
        P("phase", "dp", None),
        P(),
        P(),
        P(),
        P(),
        P(),
        P("dp"),
        P("dp", None),
    )
    return jax.shard_map(
        shards,
        mesh=mesh,
        in_specs=placed,
        out_specs=(
            P("phase", "dp", None, None),
            P("phase", "dp", None, None),
            P("phase", "dp", None, None),
            P("phase", "dp", None, None),
        ),
        check_vma=False,
    )
```

```python
import functools
import math

import jax
import jax.numpy as jnp
from jax import lax
from jax.experimental import pallas as pl
from jax.experimental.pallas import tpu as pltpu
from jax.sharding import PartitionSpec as P

HEAD_DIM = 128
TICKS = 3
WINDOW = 64
TILE = 16
GRANT = 12 * 1024 * 1024

epsilon = 1e-06

X, Y, C = 2, 4, 2


def spot(x, y, core):
    return ((x % X) * Y + (y % Y)) * C + core


def moved(value, dx, dy, dc):
    pairs = [
        (spot(x, y, c), spot(x + dx, y + dy, (c + dc) % C))
        for x in range(X)
        for y in range(Y)
        for c in range(C)
    ]
    return lax.ppermute(value, "dp", pairs)


def shifted(value):
    count = lax.axis_size("phase")
    pairs = [(source, (source + 1) % count) for source in range(count)]
    return lax.ppermute(value, "phase", pairs)


def joined(*values):
    return lax.optimization_barrier(values)


LOW, HIGH = 0, 1
NEAR = [
    [(0, 0, 0, LOW)],
    [(0, 0, 0, HIGH)],
    [(0, -1, 0, LOW)],
    [(0, 1, 0, HIGH)],
    [(1, 0, 0, LOW)],
    [(1, 0, 0, HIGH)],
    [(0, 2, 0, LOW)],
    [(0, 2, 0, HIGH)],
]
FAR = [[(1, 2, 0, LOW), (1, 2, 0, HIGH)]]
LAST = [
    [(0, -1, 0, HIGH), (1, -1, 0, LOW), (1, -1, 0, HIGH)],
    [(0, 1, 0, LOW), (1, 1, 0, LOW), (1, 1, 0, HIGH)],
]


def paired(pieces):
    return [[(dx, dy, 1, half) for dx, dy, _, half in piece] for piece in pieces]


def in_hbm(array):
    return pltpu.with_memory_space_constraint(array, pltpu.HBM)


def pair(piece):
    return moved(piece, 0, 0, 1)


def place(rows, block):
    dx, dy, dc, half = block
    device = lax.axis_index("dp")
    core = lax.rem(device % C + dc, C)
    y = lax.rem((device // C) % Y + dy + Y, Y)
    x = lax.rem(device // (C * Y) + dx, X)
    return pl.multiple_of(((x * Y + y) * C + core) * rows + half * (rows // 2), TILE)


def normalize(widened):
    return widened * lax.rsqrt(jnp.mean(widened * widened, axis=-1, keepdims=True) + epsilon)


def batch_of(tick, section, sections, lengths_ref):
    patches = lengths_ref.shape[1]
    slot = lax.rem(tick - section + sections, sections)
    picture = slot // patches
    segment = lax.rem(slot, patches)
    length = lengths_ref[picture, segment]
    offset = jnp.int32(0)
    for m in range(patches - 1):
        offset = offset + jnp.where(m < segment, lengths_ref[picture, m], 0)
    return picture, length, offset


def embedded_rows(latents, embed_w_ref, embed_b_ref, live):
    rows = jnp.dot(latents, embed_w_ref[...], preferred_element_type=jnp.float32) + embed_b_ref[...][None]
    row_ids = lax.broadcasted_iota(jnp.int32, rows.shape, 0)
    return jnp.where(row_ids < live, rows, 0.0).astype(jnp.bfloat16)


def attend(proj, image_k, image_v, text_k, text_v, attended, scores):
    width = attended.shape[1]
    tokens = text_k.shape[0]
    scale = 1.0 / math.sqrt(HEAD_DIM)
    across = (((1,), (1,)), ((), ()))
    heads = range(width // HEAD_DIM)
    columns = [slice(head * HEAD_DIM, (head + 1) * HEAD_DIM) for head in heads]
    for head in heads:
        queries = proj[:, columns[head]]
        for at, keys in enumerate((text_k, image_k)):
            scores[head, :, at * tokens : (at + 1) * tokens] = lax.dot_general(
                queries, keys[:, columns[head]], across, preferred_element_type=jnp.float32
            )
    for head in heads:
        row = scores[head]
        raised = jnp.exp((row - jnp.max(row, axis=-1, keepdims=True)) * scale)
        total = jnp.sum(raised, axis=-1, keepdims=True)
        raised = raised.astype(jnp.bfloat16)
        mixed = jnp.dot(
            raised[:, :tokens], text_v[:, columns[head]], preferred_element_type=jnp.float32
        ) + jnp.dot(raised[:, tokens:], image_v[:, columns[head]], preferred_element_type=jnp.float32)
        attended[:, columns[head]] = (mixed / total).astype(jnp.bfloat16)


def weight_copies(pieces, weights, rows, blocks, sems):
    size = rows // 2
    found = []
    for piece, held in zip(pieces, blocks):
        for at, block in enumerate(held):
            found.append(
                pltpu.make_async_copy(
                    piece.at[pl.ds(at * size, size), :],
                    weights.at[pl.ds(place(rows, block), size), :],
                    sems.at[len(found)],
                )
            )
    return found


def run_copies(copies):
    for copy in copies:
        copy.start()
    for copy in copies:
        copy.wait()


def own_kernel(qkv, out, low, high, sems):
    half, width = low.shape[0], qkv.shape[1]
    copies = []
    for at, target in enumerate((low, high)):
        rows = pl.ds(at * half, half)
        copies += [
            pltpu.make_async_copy(qkv.at[rows, :], target.at[:, pl.ds(0, width)], sems.at[2 * at]),
            pltpu.make_async_copy(
                out.at[rows, :], target.at[:, pl.ds(width, out.shape[1])], sems.at[2 * at + 1]
            ),
        ]
    run_copies(copies)


def stack_kernel(stacks, count, *refs):
    pieces, targets, sems = refs[:count], refs[count:-1], refs[-1]
    size = pieces[0].shape[0]
    copies = []
    for target, held in zip(targets, stacks):
        for at, piece in enumerate(held):
            copies.append(
                pltpu.make_async_copy(
                    pieces[piece], target.at[pl.ds(at * size, size), :], sems.at[len(copies)]
                )
            )
    run_copies(copies)


def load_kernel(rows, first, blocks, count, copied, *refs):
    if not first:
        refs = refs[1:]
    pieces, sources, refs = refs[:count], refs[count : count + copied], refs[count + copied :]
    weights, targets, refs = refs[0], refs[1 : 1 + copied], refs[1 + copied :]
    sems, copy_sems, stages = refs[0], refs[1], refs[2:]
    copies = weight_copies(pieces, weights, rows, blocks, sems)
    inward = [
        pltpu.make_async_copy(source, stage, copy_sems.at[at, 0])
        for at, (source, stage) in enumerate(zip(sources, stages))
    ]
    outward = [
        pltpu.make_async_copy(stage, target, copy_sems.at[at, 1])
        for at, (stage, target) in enumerate(zip(stages, targets))
    ]
    for copy in inward + copies:
        copy.start()
    for copy, onward in zip(inward, outward):
        copy.wait()
        onward.start()
    for copy in copies + outward:
        copy.wait()


def tick_kernel(tick, sections, first, rows, *refs):
    lengths, steps, sigmas = refs[:3]
    gain, embed_w, embed_b, head_w, head_b = refs[3:8]
    text_k, text_v, keys_in, values_in = refs[8:12]
    rest = refs[12:]
    if first:
        hidden_in, latents_in, _ = rest[:3]
        pieces = rest[3 : 3 + C * len(LAST)]
        keys, values, weights, sent, *scratch = rest[3 + C * len(LAST) :]
    else:
        received, weights = rest[:2]
        keys, values, sent, *scratch = rest[2:]
    hidden, image_k, image_v, txt_k, txt_v, proj, attended, scores, cache_sem, back_sem, *weight_sem = scratch
    width = hidden.shape[1]
    section = lax.axis_index("phase")
    picture, length, offset = batch_of(tick, section, sections, lengths)
    base = pl.multiple_of(jnp.minimum((offset // TILE) * TILE, image_k.shape[0] - WINDOW), TILE)

    loads = [
        pltpu.make_async_copy(source.at[picture], target, cache_sem.at[at])
        for at, (source, target) in enumerate(
            [(keys_in, image_k), (values_in, image_v), (text_k, txt_k), (text_v, txt_v)]
        )
    ]
    weight_loads = []
    if first:
        weight_loads = weight_copies(pieces, weights, rows, LAST + paired(LAST), weight_sem[0])
    for load in weight_loads + loads:
        load.start()

    if first:
        hidden[...] = hidden_in[...]
    else:
        hidden[...] = received[:, :width]

        @pl.when(section == 0)
        def _():
            hidden[...] = embedded_rows(
                received[:, width : width + embed_w.shape[0]], embed_w, embed_b, lengths[0, tick]
            )

    normed = (normalize(hidden[...].astype(jnp.float32)) * gain[...]).astype(jnp.bfloat16)
    for load in weight_loads:
        load.wait()
    for block in range(3):
        cols = slice(block * width, (block + 1) * width)
        proj[:, cols] = jnp.dot(normed, weights[:, cols], preferred_element_type=jnp.float32).astype(
            jnp.bfloat16
        )
    for load in loads:
        load.wait()

    token = lax.broadcasted_iota(jnp.int32, (WINDOW, proj.shape[0]), 0) + base - offset
    place = (token == lax.broadcasted_iota(jnp.int32, token.shape, 1)) & (token < length)
    place = place.astype(jnp.bfloat16)
    token = lax.broadcasted_iota(jnp.int32, (WINDOW, width), 0) + base - offset
    inside = (token >= 0) & (token < length)
    for block, cache in ((1, image_k), (2, image_v)):
        fresh = jnp.dot(
            place, proj[:, block * width : (block + 1) * width], preferred_element_type=jnp.float32
        )
        old = cache[pl.ds(base, WINDOW), :].astype(jnp.float32)
        cache[pl.ds(base, WINDOW), :] = jnp.where(inside, fresh, old).astype(jnp.bfloat16)
    backs = [
        pltpu.make_async_copy(
            source.at[pl.ds(base, WINDOW), :],
            target.at[picture, pl.ds(base, WINDOW), :],
            back_sem.at[at],
        )
        for at, (source, target) in enumerate([(image_k, keys), (image_v, values)])
    ]
    for back in backs:
        back.start()

    attend(proj, image_k, image_v, txt_k, txt_v, attended, scores)

    summed = hidden[...].astype(jnp.float32) + jnp.dot(
        attended[...], weights[:, 3 * width :], preferred_element_type=jnp.float32
    )
    row_ids = lax.broadcasted_iota(jnp.int32, summed.shape, 0)
    hidden_new = jnp.where(row_ids < length, summed, 0.0).astype(jnp.bfloat16)
    sent[:, :width] = hidden_new
    channels = embed_w.shape[0]
    latents = latents_in[...] if first else received[:, width : width + channels]
    sent[:, width:] = jnp.concatenate(
        [latents, jnp.zeros((latents.shape[0], sent.shape[1] - width - channels), latents.dtype)], axis=1
    )

    @pl.when(section == sections - 1)
    def _():
        velocity = (
            lax.dot_general(
                normalize(hidden_new.astype(jnp.float32)).astype(jnp.bfloat16),
                head_w[...],
                (((1,), (1,)), ((), ())),
                preferred_element_type=jnp.float32,
            )
            + head_b[...][None]
        )
        step = steps[picture]
        jump = sigmas[step + 1] - sigmas[step]
        stepped = latents.astype(jnp.float32) + jump * velocity
        row_ids = lax.broadcasted_iota(jnp.int32, stepped.shape, 0)
        stepped = jnp.where(row_ids < length, stepped, 0.0).astype(jnp.bfloat16)
        sent[:, width:] = jnp.concatenate(
            [stepped, jnp.zeros((latents.shape[0], sent.shape[1] - width - channels), latents.dtype)],
            axis=1,
        )

    for back in backs:
        back.wait()


def final_kernel(tick, lengths, embed_w, embed_b, received, hidden, latents):
    width = hidden.shape[1]
    arrived = received[:, width : width + latents.shape[1]]
    hidden[...] = received[:, :width]
    latents[...] = arrived

    @pl.when(lax.axis_index("phase") == 0)
    def _():
        hidden[...] = embedded_rows(arrived, embed_w, embed_b, lengths[0, tick])


def shards(
    hidden_flight,
    latent_flight,
    key_cache,
    value_cache,
    text_keys,
    text_values,
    norm_gain,
    w_qkv,
    w_out,
    embed_weight,
    embed_bias,
    head_weight,
    head_bias,
    sigma_table,
    step_index,
    patch_lengths,
):
    sections = lax.axis_size("phase")
    hidden = hidden_flight[0, 0]
    latents = latent_flight[0, 0]
    keys, values = key_cache[0], value_cache[0]
    rows, width = hidden.shape
    wide = width + HEAD_DIM
    tokens = keys.shape[1]
    part = w_qkv.shape[1]
    full = part * lax.axis_size("dp")
    smem = pl.BlockSpec(memory_space=pltpu.SMEM)
    vmem = pl.BlockSpec(memory_space=pltpu.VMEM)
    hbm = pl.BlockSpec(memory_space=pl.ANY)
    scalars = [patch_lengths, step_index, sigma_table]
    small = [norm_gain, embed_weight, embed_bias, head_weight.T, head_bias]
    texts = [text_keys[0], text_values[0]]
    params = pltpu.CompilerParams(vmem_limit_bytes=GRANT)
    small_params = pltpu.CompilerParams(vmem_limit_bytes=GRANT // 2)

    full = part * lax.axis_size("dp")
    total = w_qkv.shape[2] + w_out.shape[2]
    half = jax.ShapeDtypeStruct((part // 2, total), jnp.bfloat16)
    low, high = pl.pallas_call(
        own_kernel,
        out_shape=[half] * 2,
        in_specs=[hbm] * 2,
        out_specs=[hbm] * 2,
        scratch_shapes=[pltpu.SemaphoreType.DMA((4,))],
        compiler_params=small_params,
        name="own",
    )(in_hbm(w_qkv[0]), in_hbm(w_out[0]))

    def stacked(pieces, stacks):
        return pl.pallas_call(
            functools.partial(stack_kernel, stacks, len(pieces)),
            out_shape=[
                jax.ShapeDtypeStruct((len(held) * (part // 2), total), jnp.bfloat16) for held in stacks
            ],
            in_specs=[hbm] * len(pieces),
            out_specs=[hbm] * len(stacks),
            scratch_shapes=[pltpu.SemaphoreType.DMA((sum(len(held) for held in stacks),))],
            compiler_params=small_params,
            name="stack",
        )(*pieces)

    def loaded(name, weights, pieces, blocks, copied):
        first = weights is None
        if not first:
            weights = pltpu.with_memory_space_constraint(weights, pltpu.VMEM)
        shapes = [pltpu.VMEM((full, total), jnp.bfloat16)]
        shapes += [jax.ShapeDtypeStruct(array.shape, array.dtype) for array in copied]
        return pl.pallas_call(
            functools.partial(load_kernel, part, first, blocks, len(pieces), len(copied)),
            out_shape=shapes,
            in_specs=[vmem] * (not first) + [hbm] * (len(pieces) + len(copied)),
            out_specs=[vmem] + [hbm] * (len(shapes) - 1),
            scratch_shapes=[
                pltpu.SemaphoreType.DMA((sum(len(held) for held in blocks),)),
                pltpu.SemaphoreType.DMA((len(copied), 2)),
                *[pltpu.VMEM(array.shape, array.dtype) for array in copied],
            ],
            input_output_aliases={} if first else {0: 0},
            compiler_params=small_params,
            name=name,
        )(*([] if first else [weights]), *pieces, *[in_hbm(array) for array in copied])

    below_low, above_high = moved(low, 0, 1, 0), moved(high, 0, -1, 0)
    across_low, across_high = moved(low, 1, 0, 0), moved(high, 1, 0, 0)
    far_low, far_high = moved(below_low, 0, 1, 0), moved(above_high, 0, -1, 0)
    near = [low, high, below_low, above_high, across_low, across_high, far_low, far_high]
    near_pair, up, down, far = stacked(near, [list(range(8)), [1, 4, 5], [0, 4, 5], [6, 7]])
    near_pair = pair(near_pair)
    up, down, far = moved(up, 0, 1, 0), moved(down, 0, -1, 0), moved(far, 1, 0, 0)
    weights, keys, values = loaded(
        "near",
        None,
        [*near, near_pair],
        NEAR + [[block for piece in paired(NEAR) for block in piece]],
        [keys, values],
    )
    keys, far = joined(keys, far)
    far_pair = pair(far)
    up, down, far_pair = joined(up, down, far_pair)
    weights, latents = loaded("far", weights, [far, far_pair], FAR + paired(FAR), [latents])
    last = [up, down]
    last += [pair(piece) for piece in last]

    for tick in range(TICKS):
        first = tick == 0
        weights = pltpu.with_memory_space_constraint(weights, pltpu.VMEM)
        if first:
            own = [hidden, latents, weights] + last
            own_specs = [vmem] * 3 + [hbm] * len(last)
        else:
            own = [received, weights]
            own_specs = [vmem] * 2
        shapes = [
            jax.ShapeDtypeStruct(keys.shape, keys.dtype),
            jax.ShapeDtypeStruct(values.shape, values.dtype),
        ]
        out_specs = [hbm, hbm]
        aliases = {10: 0, 11: 1}
        if first:
            shapes.append(pltpu.VMEM(weights.shape, weights.dtype))
            out_specs.append(vmem)
            aliases[14] = 2
        shapes.append(jax.ShapeDtypeStruct((rows, wide), jnp.bfloat16))
        out_specs.append(vmem)
        scratch = [
            pltpu.VMEM((rows, width), jnp.bfloat16),
            *[pltpu.VMEM((tokens, width), jnp.bfloat16)] * 4,
            pltpu.VMEM((rows, 3 * width), jnp.bfloat16),
            pltpu.VMEM((rows, width), jnp.bfloat16),
            pltpu.VMEM((width // HEAD_DIM, rows, 2 * tokens), jnp.float32),
            pltpu.SemaphoreType.DMA((4,)),
            pltpu.SemaphoreType.DMA((2,)),
        ]
        if first:
            scratch.append(pltpu.SemaphoreType.DMA((2 * sum(len(held) for held in LAST),)))
        results = pl.pallas_call(
            functools.partial(tick_kernel, tick, sections, first, part),
            out_shape=shapes,
            in_specs=[smem] * 3 + [vmem] * 5 + [hbm] * 4 + own_specs,
            out_specs=out_specs,
            scratch_shapes=scratch,
            input_output_aliases=aliases,
            compiler_params=params,
            name=f"tick{tick}",
        )(*scalars, *small, *texts, keys, values, *own)
        if first:
            keys, values, weights, sent = results
        else:
            keys, values, sent = results
        received = shifted(sent)

    hidden, latents = pl.pallas_call(
        functools.partial(final_kernel, TICKS),
        out_shape=[
            jax.ShapeDtypeStruct(hidden.shape, hidden.dtype),
            jax.ShapeDtypeStruct(latents.shape, latents.dtype),
        ],
        in_specs=[smem, vmem, vmem, vmem],
        out_specs=[vmem, vmem],
        compiler_params=params,
        name="final",
    )(patch_lengths, embed_weight, embed_bias, received)
    return (hidden[None, None], latents[None, None], keys[None], values[None])


def solution(mesh):
    placed = (
        P("phase", "dp", None, None),
        P("phase", "dp", None, None),
        P("phase", "dp", None, None),
        P("phase", "dp", None, None),
        P("phase", "dp", None, None),
        P("phase", "dp", None, None),
        P("phase", None),
        P("phase", "dp", None),
        P("phase", "dp", None),
        P(),
        P(),
        P(),
        P(),
        P(),
        P("dp"),
        P("dp", None),
    )
    return jax.shard_map(
        shards,
        mesh=mesh,
        in_specs=placed,
        out_specs=(
            P("phase", "dp", None, None),
            P("phase", "dp", None, None),
            P("phase", "dp", None, None),
            P("phase", "dp", None, None),
        ),
        check_vma=False,
    )
```

```python
import functools
import math

import jax
import jax.numpy as jnp
from jax import lax
from jax.experimental import pallas as pl
from jax.experimental.pallas import tpu as pltpu
from jax.sharding import PartitionSpec as P

HEAD_DIM = 128
TICKS = 3
WINDOW = 64
TILE = 16
GRANT = 12 * 1024 * 1024

epsilon = 1e-06

X, Y, C = 2, 4, 2


def spot(x, y, core):
    return ((x % X) * Y + (y % Y)) * C + core


def moved(value, dx, dy, dc):
    pairs = [
        (spot(x, y, c), spot(x + dx, y + dy, (c + dc) % C))
        for x in range(X)
        for y in range(Y)
        for c in range(C)
    ]
    return lax.ppermute(value, "dp", pairs)


def shifted(value):
    count = lax.axis_size("phase")
    pairs = [(source, (source + 1) % count) for source in range(count)]
    return lax.ppermute(value, "phase", pairs)


def joined(*values):
    return lax.optimization_barrier(values)


NEAR = [
    [(0, 0, 0, 0, 3)],
    [(0, 0, 0, 3, 3)],
    [(0, -1, 0, 0, 3)],
    [(0, 1, 0, 3, 3)],
    [(1, 0, 0, 0, 3)],
    [(1, 0, 0, 3, 3)],
    [(0, 2, 0, 0, 3)],
    [(0, 2, 0, 3, 3)],
]
FAR = [[(1, 2, 0, 0, 3), (1, 2, 0, 3, 3)], [(1, -1, 0, 0, 1), (1, 1, 0, 5, 1)]]
LAST = [
    [(0, -1, 0, 3, 3), (1, -1, 0, 1, 5)],
    [(0, 1, 0, 0, 3), (1, 1, 0, 0, 5)],
]


def paired(pieces):
    return [[(dx, dy, 1, first, tiles) for dx, dy, _, first, tiles in piece] for piece in pieces]


def in_hbm(array):
    return pltpu.with_memory_space_constraint(array, pltpu.HBM)


def pair(piece):
    return moved(piece, 0, 0, 1)


def place(rows, block):
    dx, dy, dc, first, _ = block
    device = lax.axis_index("dp")
    core = lax.rem(device % C + dc, C)
    y = lax.rem((device // C) % Y + dy + Y, Y)
    x = lax.rem(device // (C * Y) + dx, X)
    return pl.multiple_of(((x * Y + y) * C + core) * rows + first * TILE, TILE)


def normalize(widened):
    return widened * lax.rsqrt(jnp.mean(widened * widened, axis=-1, keepdims=True) + epsilon)


def batch_of(tick, section, sections, lengths_ref):
    patches = lengths_ref.shape[1]
    slot = lax.rem(tick - section + sections, sections)
    picture = slot // patches
    segment = lax.rem(slot, patches)
    length = lengths_ref[picture, segment]
    offset = jnp.int32(0)
    for m in range(patches - 1):
        offset = offset + jnp.where(m < segment, lengths_ref[picture, m], 0)
    return picture, length, offset


def embedded_rows(latents, embed_w_ref, embed_b_ref, live):
    rows = jnp.dot(latents, embed_w_ref[...], preferred_element_type=jnp.float32) + embed_b_ref[...][None]
    row_ids = lax.broadcasted_iota(jnp.int32, rows.shape, 0)
    return jnp.where(row_ids < live, rows, 0.0).astype(jnp.bfloat16)


def attend(proj, image_k, image_v, text_k, text_v, attended, scores):
    width = attended.shape[1]
    tokens = text_k.shape[0]
    scale = 1.0 / math.sqrt(HEAD_DIM)
    across = (((1,), (1,)), ((), ()))
    heads = range(width // HEAD_DIM)
    columns = [slice(head * HEAD_DIM, (head + 1) * HEAD_DIM) for head in heads]
    for head in heads:
        queries = proj[:, columns[head]]
        for at, keys in enumerate((text_k, image_k)):
            scores[head, :, at * tokens : (at + 1) * tokens] = lax.dot_general(
                queries, keys[:, columns[head]], across, preferred_element_type=jnp.float32
            )
    for head in heads:
        row = scores[head]
        raised = jnp.exp((row - jnp.max(row, axis=-1, keepdims=True)) * scale)
        total = jnp.sum(raised, axis=-1, keepdims=True)
        raised = raised.astype(jnp.bfloat16)
        mixed = jnp.dot(
            raised[:, :tokens], text_v[:, columns[head]], preferred_element_type=jnp.float32
        ) + jnp.dot(raised[:, tokens:], image_v[:, columns[head]], preferred_element_type=jnp.float32)
        attended[:, columns[head]] = (mixed / total).astype(jnp.bfloat16)


def weight_copies(pieces, weights, rows, blocks, sems):
    found = []
    for piece, held in zip(pieces, blocks):
        start = 0
        for block in held:
            size = block[-1] * TILE
            found.append(
                pltpu.make_async_copy(
                    piece.at[pl.ds(start, size), :],
                    weights.at[pl.ds(place(rows, block), size), :],
                    sems.at[len(found)],
                )
            )
            start += size
    return found


def run_copies(copies):
    for copy in copies:
        copy.start()
    for copy in copies:
        copy.wait()


def own_kernel(qkv, out, low, high, sems):
    half, width = low.shape[0], qkv.shape[1]
    copies = []
    for at, target in enumerate((low, high)):
        rows = pl.ds(at * half, half)
        copies += [
            pltpu.make_async_copy(qkv.at[rows, :], target.at[:, pl.ds(0, width)], sems.at[2 * at]),
            pltpu.make_async_copy(
                out.at[rows, :], target.at[:, pl.ds(width, out.shape[1])], sems.at[2 * at + 1]
            ),
        ]
    run_copies(copies)


def stack_kernel(stacks, count, *refs):
    pieces, targets, sems = refs[:count], refs[count:-1], refs[-1]
    copies = []
    for target, held in zip(targets, stacks):
        start = 0
        for piece, first, tiles in held:
            copies.append(
                pltpu.make_async_copy(
                    pieces[piece].at[pl.ds(first * TILE, tiles * TILE), :],
                    target.at[pl.ds(start, tiles * TILE), :],
                    sems.at[len(copies)],
                )
            )
            start += tiles * TILE
    run_copies(copies)


def load_kernel(rows, first, blocks, count, copied, *refs):
    if not first:
        refs = refs[1:]
    pieces, sources, refs = refs[:count], refs[count : count + copied], refs[count + copied :]
    weights, targets, refs = refs[0], refs[1 : 1 + copied], refs[1 + copied :]
    sems, copy_sems, stages = refs[0], refs[1], refs[2:]
    copies = weight_copies(pieces, weights, rows, blocks, sems)
    inward = [
        pltpu.make_async_copy(source, stage, copy_sems.at[at, 0])
        for at, (source, stage) in enumerate(zip(sources, stages))
    ]
    outward = [
        pltpu.make_async_copy(stage, target, copy_sems.at[at, 1])
        for at, (stage, target) in enumerate(zip(stages, targets))
    ]
    for copy in inward + copies:
        copy.start()
    for copy, onward in zip(inward, outward):
        copy.wait()
        onward.start()
    for copy in copies + outward:
        copy.wait()


def tick_kernel(tick, sections, first, rows, *refs):
    lengths, steps, sigmas = refs[:3]
    gain, embed_w, embed_b, head_w, head_b = refs[3:8]
    text_k, text_v, keys_in, values_in = refs[8:12]
    rest = refs[12:]
    if first:
        hidden_in, latents_in, _ = rest[:3]
        pieces = rest[3 : 3 + C * len(LAST)]
        keys, values, weights, sent, *scratch = rest[3 + C * len(LAST) :]
    else:
        received, weights = rest[:2]
        keys, values, sent, *scratch = rest[2:]
    hidden, image_k, image_v, txt_k, txt_v, proj, attended, scores, cache_sem, back_sem, *weight_sem = scratch
    width = hidden.shape[1]
    section = lax.axis_index("phase")
    picture, length, offset = batch_of(tick, section, sections, lengths)
    base = pl.multiple_of(jnp.minimum((offset // TILE) * TILE, image_k.shape[0] - WINDOW), TILE)

    loads = [
        pltpu.make_async_copy(source.at[picture], target, cache_sem.at[at])
        for at, (source, target) in enumerate(
            [(keys_in, image_k), (values_in, image_v), (text_k, txt_k), (text_v, txt_v)]
        )
    ]
    weight_loads = []
    if first:
        weight_loads = weight_copies(pieces, weights, rows, LAST + paired(LAST), weight_sem[0])
    for load in weight_loads + loads:
        load.start()

    if first:
        hidden[...] = hidden_in[...]
    else:
        hidden[...] = received[:, :width]

        @pl.when(section == 0)
        def _():
            hidden[...] = embedded_rows(
                received[:, width : width + embed_w.shape[0]], embed_w, embed_b, lengths[0, tick]
            )

    normed = (normalize(hidden[...].astype(jnp.float32)) * gain[...]).astype(jnp.bfloat16)
    for load in weight_loads:
        load.wait()
    for block in range(3):
        cols = slice(block * width, (block + 1) * width)
        proj[:, cols] = jnp.dot(normed, weights[:, cols], preferred_element_type=jnp.float32).astype(
            jnp.bfloat16
        )
    for load in loads:
        load.wait()

    token = lax.broadcasted_iota(jnp.int32, (WINDOW, proj.shape[0]), 0) + base - offset
    place = (token == lax.broadcasted_iota(jnp.int32, token.shape, 1)) & (token < length)
    place = place.astype(jnp.bfloat16)
    token = lax.broadcasted_iota(jnp.int32, (WINDOW, width), 0) + base - offset
    inside = (token >= 0) & (token < length)
    for block, cache in ((1, image_k), (2, image_v)):
        fresh = jnp.dot(
            place, proj[:, block * width : (block + 1) * width], preferred_element_type=jnp.float32
        )
        old = cache[pl.ds(base, WINDOW), :].astype(jnp.float32)
        cache[pl.ds(base, WINDOW), :] = jnp.where(inside, fresh, old).astype(jnp.bfloat16)
    backs = [
        pltpu.make_async_copy(
            source.at[pl.ds(base, WINDOW), :],
            target.at[picture, pl.ds(base, WINDOW), :],
            back_sem.at[at],
        )
        for at, (source, target) in enumerate([(image_k, keys), (image_v, values)])
    ]
    for back in backs:
        back.start()

    attend(proj, image_k, image_v, txt_k, txt_v, attended, scores)

    summed = hidden[...].astype(jnp.float32) + jnp.dot(
        attended[...], weights[:, 3 * width :], preferred_element_type=jnp.float32
    )
    row_ids = lax.broadcasted_iota(jnp.int32, summed.shape, 0)
    hidden_new = jnp.where(row_ids < length, summed, 0.0).astype(jnp.bfloat16)
    sent[:, :width] = hidden_new
    channels = embed_w.shape[0]
    latents = latents_in[...] if first else received[:, width : width + channels]
    sent[:, width:] = jnp.concatenate(
        [latents, jnp.zeros((latents.shape[0], sent.shape[1] - width - channels), latents.dtype)], axis=1
    )

    @pl.when(section == sections - 1)
    def _():
        velocity = (
            lax.dot_general(
                normalize(hidden_new.astype(jnp.float32)).astype(jnp.bfloat16),
                head_w[...],
                (((1,), (1,)), ((), ())),
                preferred_element_type=jnp.float32,
            )
            + head_b[...][None]
        )
        step = steps[picture]
        jump = sigmas[step + 1] - sigmas[step]
        stepped = latents.astype(jnp.float32) + jump * velocity
        row_ids = lax.broadcasted_iota(jnp.int32, stepped.shape, 0)
        stepped = jnp.where(row_ids < length, stepped, 0.0).astype(jnp.bfloat16)
        sent[:, width:] = jnp.concatenate(
            [stepped, jnp.zeros((latents.shape[0], sent.shape[1] - width - channels), latents.dtype)],
            axis=1,
        )

    for back in backs:
        back.wait()


def final_kernel(tick, lengths, embed_w, embed_b, received, hidden, latents):
    width = hidden.shape[1]
    arrived = received[:, width : width + latents.shape[1]]
    hidden[...] = received[:, :width]
    latents[...] = arrived

    @pl.when(lax.axis_index("phase") == 0)
    def _():
        hidden[...] = embedded_rows(arrived, embed_w, embed_b, lengths[0, tick])


def shards(
    hidden_flight,
    latent_flight,
    key_cache,
    value_cache,
    text_keys,
    text_values,
    norm_gain,
    w_qkv,
    w_out,
    embed_weight,
    embed_bias,
    head_weight,
    head_bias,
    sigma_table,
    step_index,
    patch_lengths,
):
    sections = lax.axis_size("phase")
    hidden = hidden_flight[0, 0]
    latents = latent_flight[0, 0]
    keys, values = key_cache[0], value_cache[0]
    rows, width = hidden.shape
    wide = width + HEAD_DIM
    tokens = keys.shape[1]
    part = w_qkv.shape[1]
    full = part * lax.axis_size("dp")
    smem = pl.BlockSpec(memory_space=pltpu.SMEM)
    vmem = pl.BlockSpec(memory_space=pltpu.VMEM)
    hbm = pl.BlockSpec(memory_space=pl.ANY)
    scalars = [patch_lengths, step_index, sigma_table]
    small = [norm_gain, embed_weight, embed_bias, head_weight.T, head_bias]
    texts = [text_keys[0], text_values[0]]
    params = pltpu.CompilerParams(vmem_limit_bytes=GRANT)
    small_params = pltpu.CompilerParams(vmem_limit_bytes=GRANT // 2)

    full = part * lax.axis_size("dp")
    total = w_qkv.shape[2] + w_out.shape[2]
    half = jax.ShapeDtypeStruct((part // 2, total), jnp.bfloat16)
    low, high = pl.pallas_call(
        own_kernel,
        out_shape=[half] * 2,
        in_specs=[hbm] * 2,
        out_specs=[hbm] * 2,
        scratch_shapes=[pltpu.SemaphoreType.DMA((4,))],
        compiler_params=small_params,
        name="own",
    )(in_hbm(w_qkv[0]), in_hbm(w_out[0]))

    def stacked(pieces, stacks):
        return pl.pallas_call(
            functools.partial(stack_kernel, stacks, len(pieces)),
            out_shape=[
                jax.ShapeDtypeStruct((sum(tiles for *_, tiles in held) * TILE, total), jnp.bfloat16)
                for held in stacks
            ],
            in_specs=[hbm] * len(pieces),
            out_specs=[hbm] * len(stacks),
            scratch_shapes=[pltpu.SemaphoreType.DMA((sum(len(held) for held in stacks),))],
            compiler_params=small_params,
            name="stack",
        )(*pieces)

    def loaded(name, weights, pieces, blocks, copied):
        first = weights is None
        if not first:
            weights = pltpu.with_memory_space_constraint(weights, pltpu.VMEM)
        shapes = [pltpu.VMEM((full, total), jnp.bfloat16)]
        shapes += [jax.ShapeDtypeStruct(array.shape, array.dtype) for array in copied]
        return pl.pallas_call(
            functools.partial(load_kernel, part, first, blocks, len(pieces), len(copied)),
            out_shape=shapes,
            in_specs=[vmem] * (not first) + [hbm] * (len(pieces) + len(copied)),
            out_specs=[vmem] + [hbm] * (len(shapes) - 1),
            scratch_shapes=[
                pltpu.SemaphoreType.DMA((sum(len(held) for held in blocks),)),
                pltpu.SemaphoreType.DMA((len(copied), 2)),
                *[pltpu.VMEM(array.shape, array.dtype) for array in copied],
            ],
            input_output_aliases={} if first else {0: 0},
            compiler_params=small_params,
            name=name,
        )(*([] if first else [weights]), *pieces, *[in_hbm(array) for array in copied])

    below_low, above_high = moved(low, 0, 1, 0), moved(high, 0, -1, 0)
    across_low, across_high = moved(low, 1, 0, 0), moved(high, 1, 0, 0)
    far_low, far_high = moved(below_low, 0, 1, 0), moved(above_high, 0, -1, 0)
    near = [low, high, below_low, above_high, across_low, across_high, far_low, far_high]
    near_pair, up, down, far, side = stacked(
        near,
        [
            [(piece, 0, 3) for piece in range(len(near))],
            [(1, 0, 3), (4, 1, 2), (5, 0, 3)],
            [(0, 0, 3), (4, 0, 3), (5, 0, 2)],
            [(6, 0, 3), (7, 0, 3)],
            [(2, 0, 1), (3, 2, 1)],
        ],
    )
    near_pair = pair(near_pair)
    up, down = moved(up, 0, 1, 0), moved(down, 0, -1, 0)
    far, side = moved(far, 1, 0, 0), moved(side, 1, 0, 0)
    weights, keys, values = loaded(
        "near",
        None,
        [*near, near_pair],
        NEAR + [[block for piece in paired(NEAR) for block in piece]],
        [keys, values],
    )
    keys, far, side = joined(keys, far, side)
    far_pair, side_pair = pair(far), pair(side)
    up, down, far_pair, side_pair = joined(up, down, far_pair, side_pair)
    weights, latents = loaded("far", weights, [far, side, far_pair, side_pair], FAR + paired(FAR), [latents])
    last = [up, down]
    last += [pair(piece) for piece in last]

    for tick in range(TICKS):
        first = tick == 0
        weights = pltpu.with_memory_space_constraint(weights, pltpu.VMEM)
        if first:
            own = [hidden, latents, weights] + last
            own_specs = [vmem] * 3 + [hbm] * len(last)
        else:
            own = [received, weights]
            own_specs = [vmem] * 2
        shapes = [
            jax.ShapeDtypeStruct(keys.shape, keys.dtype),
            jax.ShapeDtypeStruct(values.shape, values.dtype),
        ]
        out_specs = [hbm, hbm]
        aliases = {10: 0, 11: 1}
        if first:
            shapes.append(pltpu.VMEM(weights.shape, weights.dtype))
            out_specs.append(vmem)
            aliases[14] = 2
        shapes.append(jax.ShapeDtypeStruct((rows, wide), jnp.bfloat16))
        out_specs.append(vmem)
        scratch = [
            pltpu.VMEM((rows, width), jnp.bfloat16),
            *[pltpu.VMEM((tokens, width), jnp.bfloat16)] * 4,
            pltpu.VMEM((rows, 3 * width), jnp.bfloat16),
            pltpu.VMEM((rows, width), jnp.bfloat16),
            pltpu.VMEM((width // HEAD_DIM, rows, 2 * tokens), jnp.float32),
            pltpu.SemaphoreType.DMA((4,)),
            pltpu.SemaphoreType.DMA((2,)),
        ]
        if first:
            scratch.append(pltpu.SemaphoreType.DMA((2 * sum(len(held) for held in LAST),)))
        results = pl.pallas_call(
            functools.partial(tick_kernel, tick, sections, first, part),
            out_shape=shapes,
            in_specs=[smem] * 3 + [vmem] * 5 + [hbm] * 4 + own_specs,
            out_specs=out_specs,
            scratch_shapes=scratch,
            input_output_aliases=aliases,
            compiler_params=params,
            name=f"tick{tick}",
        )(*scalars, *small, *texts, keys, values, *own)
        if first:
            keys, values, weights, sent = results
        else:
            keys, values, sent = results
        received = shifted(sent)

    hidden, latents = pl.pallas_call(
        functools.partial(final_kernel, TICKS),
        out_shape=[
            jax.ShapeDtypeStruct(hidden.shape, hidden.dtype),
            jax.ShapeDtypeStruct(latents.shape, latents.dtype),
        ],
        in_specs=[smem, vmem, vmem, vmem],
        out_specs=[vmem, vmem],
        compiler_params=params,
        name="final",
    )(patch_lengths, embed_weight, embed_bias, received)
    return (hidden[None, None], latents[None, None], keys[None], values[None])


def solution(mesh):
    placed = (
        P("phase", "dp", None, None),
        P("phase", "dp", None, None),
        P("phase", "dp", None, None),
        P("phase", "dp", None, None),
        P("phase", "dp", None, None),
        P("phase", "dp", None, None),
        P("phase", None),
        P("phase", "dp", None),
        P("phase", "dp", None),
        P(),
        P(),
        P(),
        P(),
        P(),
        P("dp"),
        P("dp", None),
    )
    return jax.shard_map(
        shards,
        mesh=mesh,
        in_specs=placed,
        out_specs=(
            P("phase", "dp", None, None),
            P("phase", "dp", None, None),
            P("phase", "dp", None, None),
            P("phase", "dp", None, None),
        ),
        check_vma=False,
    )
```
